512 devices in a mesh: section: 16 (over y, x_hi), dp: 32 (over z, x_lo, core).
Axes of the slice: x: 4 (x_hi: 2, x_lo: 2; x = x_hi * 2 + x_lo), y: 8, z: 8, core: 2. Of those that a mesh axis runs over, the one named last changes fastest.
Arguments:
- saved_states: bfloat16 [16, 2, 128, 2688], P('section', None, 'dp'), may hold values from -64 to 64
- cotangent_in: bfloat16 [16, 128, 2688], P('section', 'dp'), may hold values from -6 to 6
- lengths: int32 [16], P('section'), may hold values from 16 to 128
- gain: bfloat16 [2688], replicated, may hold values from 0.099609375 to 1.8984375
- up_weight: bfloat16 [2688, 9216], P('section', 'dp'), may hold values from -0.125 to 0.125
- down_weight: bfloat16 [9216, 2688], P('dp', 'section'), may hold values from -0.0625 to 0.0625
Outputs:
- cotangent_out: bfloat16 [16, 128, 2688], P('section', 'dp')
- up_gradient: bfloat16 [2688, 9216], P('section', 'dp')
- down_gradient: bfloat16 [9216, 2688], P('dp', 'section')
- gain_gradient: float32 [2688], replicated
The draws below stay inside these ranges and needn't reach their ends.
All inputs are finite; a program needn't handle non-finite values.
Results may differ from the reference program's by a relative error of at most 0.024.
Values may be sent and summed in bfloat16 or wider, within the bound.
A program may use at most 64 MiB of HBM per device.

```python
import math
import jax
import jax.numpy as jnp
from jax import lax

D = 2688
F = 9216
TOK = 128
MICRO = 2
SECTIONS = 16
HIDDEN_BLOCKS = 32
LAP_TOKENS = 4096


def draw_saved_states(key, part):
    first, second, third = jax.random.split(jax.random.fold_in(key, 11), 3)
    shape = (SECTIONS, MICRO, TOK, D)
    row_scale = jnp.exp(jax.random.uniform(second, (SECTIONS, MICRO, TOK, 1), jnp.float32, 0.0, math.log(10.0)))
    column_scale = jnp.exp(jax.random.uniform(third, (D,), jnp.float32, math.log(0.5), math.log(5.0)))
    base = jax.random.normal(first, shape, jnp.float32)
    return jnp.clip(base * row_scale * column_scale, -64.0, 64.0).astype(jnp.bfloat16)


def draw_lengths(key, part):
    first, second, third = jax.random.split(jax.random.fold_in(key, 23), 3)
    values = jax.random.randint(first, (SECTIONS,), TOK // 8, TOK + 1)
    highest = jax.random.randint(second, (), 0, SECTIONS)
    lowest = (highest + jax.random.randint(third, (), 1, SECTIONS)) % SECTIONS
    places = jnp.arange(SECTIONS)
    values = jnp.where(places == highest, TOK, jnp.where(places == lowest, TOK // 8, values))
    return values.astype(jnp.int32)


def shard_levels(stream_key, dims, cuts, smallest, high):
    loudness, own = 1.0, jax.random.fold_in(stream_key, 6)
    for axis_at, blocks in cuts:
        steps = jnp.exp(jax.random.uniform(jax.random.fold_in(own, axis_at), (blocks,), jnp.float32, smallest / len(cuts), high / len(cuts)))
        loudness = loudness * jnp.repeat(steps, dims[axis_at] // blocks).reshape([-1 if axis == axis_at else 1 for axis in range(len(dims))])
    return loudness


def centred(key, shape, deviation, most, cuts=(), kind=jnp.bfloat16):
    entries = jax.random.normal(key, shape, jnp.float32) * deviation
    if len(cuts) > 0:
        entries = shard_levels(key, shape, cuts, -0.22, 0.18) * entries
    return jnp.clip(entries, min=-most, max=most).astype(kind)


def setup_inputs(seed: int = 0) -> dict:
    key_of = jax.random.split(jax.random.key(seed), 7)
    return {
        "saved_states": draw_saved_states(jax.random.fold_in(key_of[6], 71), 0),
        "cotangent_in": centred(key_of[1], (SECTIONS, TOK, D), 1.0, 6.0, ((0, 16), (1, 32))),
        "lengths": draw_lengths(jax.random.fold_in(key_of[6], 71), 0),
        "gain": jnp.clip(1.0 + 0.18 * jax.random.normal(key_of[3], (D,), jnp.float32), 0.099609375, 1.8984375).astype(jnp.bfloat16),
        "up_weight": centred(key_of[4], (D, F), D ** -0.5, 0.125, ((0, 16), (1, 32))),
        "down_weight": centred(key_of[5], (F, D), F ** -0.5, 0.0625, ((0, 32), (1, 16))),
    }


epsilon = 1e-06

def back_iteration(state, cotangent, gain, up_weight, down_weight, with_terms):
    values = state.astype(jnp.float32)
    reciprocal = lax.rsqrt(lax.optimization_barrier(jnp.mean(values * values, axis=-1, keepdims=True)) + epsilon)
    scaled = values * reciprocal
    gain_wide = gain.astype(jnp.float32)
    normed = (scaled * gain_wide).astype(jnp.bfloat16)
    hidden_in = jnp.dot(normed, up_weight, preferred_element_type=jnp.float32)
    sigma = jax.nn.sigmoid(hidden_in)
    hidden_out = (hidden_in * sigma).astype(jnp.bfloat16)
    back_out = lax.dot_general(cotangent, down_weight, (((1,), (1,)), ((), ())), preferred_element_type=jnp.float32)
    back_in = (back_out * sigma * (1.0 + hidden_in * (1.0 - sigma))).astype(jnp.bfloat16)
    tokens = back_in.shape[0]
    blocked = back_in.astype(jnp.float32).reshape(tokens, HIDDEN_BLOCKS, -1)
    weights_blocked = up_weight.astype(jnp.float32).reshape(up_weight.shape[0], HIDDEN_BLOCKS, -1)
    partials = jnp.einsum('tgf,dgf->gtd', blocked, weights_blocked)
    rounded = lax.optimization_barrier(partials.astype(jnp.bfloat16))
    back_normed = lax.optimization_barrier(jnp.sum(rounded.astype(jnp.float32), axis=0))
    gained = back_normed * gain_wide
    back_state = reciprocal * (gained - scaled * lax.optimization_barrier(jnp.mean(gained * scaled, axis=-1, keepdims=True)))
    result = (cotangent.astype(jnp.float32) + back_state).astype(jnp.bfloat16)
    if not with_terms:
        return result
    gain_term = lax.optimization_barrier(jnp.sum(back_normed * scaled, axis=0))
    up_term = lax.dot_general(normed, back_in, (((0,), (0,)), ((), ())), preferred_element_type=jnp.float32)
    down_term = lax.dot_general(hidden_out, cotangent, (((0,), (0,)), ((), ())), preferred_element_type=jnp.float32)
    return (result, up_term, down_term, gain_term)

def reference(saved_states, cotangent_in, lengths, gain, up_weight, down_weight):
    positions = jnp.arange(TOK, dtype=jnp.int32)
    keep = positions[None, :, None] < lengths.astype(jnp.int32)[:, None, None]
    masked = jnp.where(keep, cotangent_in, jnp.zeros_like(cotangent_in))

    def carry_only(inputs):
        state, cotangent = inputs
        return back_iteration(state, cotangent, gain, up_weight, down_weight, False)
    flows = [masked]
    for turn in range(MICRO - 1):
        moved = lax.map(carry_only, (saved_states[:, turn], flows[-1]))
        flows.append(jnp.roll(moved, -1, axis=0))
    stacked = jnp.stack(flows, axis=1)
    scale = 1.0 / math.sqrt(LAP_TOKENS)

    def section_sum(carry, inputs):
        states, cotangents = inputs
        up_total, down_total, gain_total = carry
        up_section = jnp.zeros(up_weight.shape, jnp.float32)
        down_section = jnp.zeros(down_weight.shape, jnp.float32)
        result = cotangents[0]
        for turn in range(MICRO):
            result, up_term, down_term, gain_term = back_iteration(states[turn], cotangents[turn], gain, up_weight, down_weight, True)
            up_section = up_section + up_term
            down_section = down_section + down_term
            gain_total = gain_total + gain_term * scale
        up_part = lax.optimization_barrier((up_section * scale).astype(jnp.bfloat16))
        down_part = lax.optimization_barrier((down_section * scale).astype(jnp.bfloat16))
        up_total = up_total + up_part.astype(jnp.float32)
        down_total = down_total + down_part.astype(jnp.float32)
        return ((up_total, down_total, gain_total), result)
    start = (jnp.zeros(up_weight.shape, jnp.float32), jnp.zeros(down_weight.shape, jnp.float32), jnp.zeros((D,), jnp.float32))
    totals, outputs = lax.scan(section_sum, start, (saved_states, stacked))
    up_total, down_total, gain_total = totals
    return (outputs, up_total.astype(jnp.bfloat16), down_total.astype(jnp.bfloat16), gain_total)
```

```python
import functools
import math

import jax
import jax.numpy as jnp
from jax import lax
from jax.experimental import pallas as pl
from jax.experimental.pallas import tpu as pltpu
from jax.sharding import PartitionSpec as P

MESH = pl.DeviceIdType.MESH
F32, BF16 = jnp.float32, jnp.bfloat16
epsilon = 1e-06

Y_ITEMS = {
    1: ((0, 0), (1, 0), (0, 1), (1, 1), (0, 2), (1, 2), (0, 3)),
    -1: ((0, 0), (1, 0), (0, 1), (1, 1), (0, 2), (1, 2), (1, 3)),
}
G_ITEMS = {
    1: ((0, 4), (1, 3), (0, 3), (1, 2), (0, 2), (1, 1), (0, 1)),
    -1: ((1, 4), (0, 3), (1, 3), (0, 2), (1, 2), (0, 1), (1, 1)),
}
Z_REACH = {1: 4, -1: 3}
DIRS = (1, -1)


def mod(a, n):
    return lax.rem(a + n, n)


def dot(a, b):
    return jnp.dot(a, b, preferred_element_type=F32)


def dot_t(a, b):
    return lax.dot_general(a, b, (((1,), (1,)), ((), ())), preferred_element_type=F32)


def kernel(
    scale, states, cot_in, lengths, gain, up, down,
    cot_out, up_out, down_out, gain_out,
    w, e_s, e_c, acts, cots, xn, xc, bm, hm, br, hr,
    pb, rc, qb, rz, st, sr, res, gs, gr, fs, fr,
    ga, gz, gy, send, recv,
):
    s, p = lax.axis_index("section"), lax.axis_index("dp")
    y, h = lax.div(s, 2), lax.rem(s, 2)
    z, l, c = lax.div(p, 4), lax.rem(lax.div(p, 2), 2), lax.rem(p, 2)
    g = 1 - h

    def at(section=None, dp=None):
        return {"section": s if section is None else section, "dp": p if dp is None else dp}

    def at_y(k):
        return at(section=mod(y + k, 8) * 2 + h)

    def at_z(k):
        return at(dp=mod(z + k, 8) * 4 + l * 2 + c)

    pair_h = at(section=s + 1 - 2 * h)
    pair_l = at(dp=p + 2 - 4 * l)
    pair_c = at(dp=p + 1 - 2 * c)
    before = at(section=mod(s - 1, 16))
    cross = at(section=mod(s - 1 + 2 * h, 16))

    count = [0]

    class Copy:
        def __init__(self, src, dst, landing, device):
            k = count[0]
            count[0] += 1
            self.out = pltpu.make_async_remote_copy(
                src_ref=src, dst_ref=dst, send_sem=send.at[k], recv_sem=recv.at[k],
                device_id=device, device_id_type=MESH,
            )
            self.arrival = pltpu.make_async_remote_copy(
                src_ref=src, dst_ref=landing, send_sem=send.at[k], recv_sem=recv.at[k],
                device_id=device, device_id_type=MESH,
            )
            pending.append(self)
            self.out.start()

        def arrived(self):
            self.arrival.wait_recv()

    pending = []

    barrier = pltpu.get_barrier_semaphore()
    partners = [at_y(k) for k in range(1, 8)] + [at_z(k) for k in range(1, 8)]
    partners += [pair_h, pair_l, pair_c, cross]
    for device in partners:
        pl.semaphore_signal(barrier, inc=1, device_id=device, device_id_type=MESH)

    down_t = down[...].astype(F32).T
    up_own = up[...].astype(F32)
    rows = up_own.shape[0]
    w[y, h, :, 0:256] = up_own[:, 0:256].astype(BF16)
    w[y, h, :, 256:512] = down_t[:, 0:256].astype(BF16)
    w[y, h, :, 512:640] = jnp.concatenate(
        [up_own[:, 256:288], down_t[:, 256:288], jnp.zeros((rows, 64), F32)], axis=1
    ).astype(BF16)
    e_s[l] = states[0]
    e_c[l] = cot_in[0]

    pl.semaphore_wait(barrier, len(partners))

    swap_s = Copy(e_s.at[l], e_s.at[l], e_s.at[1 - l], pair_l)
    swap_c = Copy(e_c.at[l], e_c.at[l], e_c.at[1 - l], pair_l)
    swap_w = Copy(w.at[y, h], w.at[y, h], w.at[y, g], pair_h)

    y_copies = {}

    def y_step(i):
        for way in DIRS:
            sub, far = Y_ITEMS[way][i]
            if far > 0:
                y_copies[way, sub, far - 1].arrived()
            elif sub == 1 and way == 1:
                swap_w.arrived()
            row = mod(y - way * far, 8)
            land = mod(y - way * (far + 1), 8)
            at_h = g if sub else h
            y_copies[way, sub, far] = Copy(w.at[row, at_h], w.at[row, at_h], w.at[land, at_h], at_y(way))

    y_step(0)

    gain_wide = gain[...].astype(F32)
    swap_s.arrived()
    swap_c.arrived()
    in_chunk = lax.broadcasted_iota(jnp.int32, (8, 1), 0)
    position = z * 16 + c * 4 + jnp.where(in_chunk >= 4, in_chunk + 4, in_chunk)
    d = gain_wide.shape[1]

    def own_state(m):
        values = jnp.concatenate([e_s[0, m].astype(F32), e_s[1, m].astype(F32)], axis=0)
        reciprocal = lax.rsqrt(jnp.mean(values * values, axis=-1, keepdims=True) + epsilon)
        return values * reciprocal, reciprocal

    for m in range(2):
        acts[m, z, c] = (own_state(m)[0] * gain_wide).astype(BF16)
    raw = jnp.concatenate([e_c[0].astype(F32), e_c[1].astype(F32)], axis=0)
    acts[2, z, c] = jnp.where(position < lengths[0], raw, 0.0).astype(BF16)

    z_copies, c_copies = {}, []

    def to_core(row):
        c_copies.append(
            Copy(acts.at[:, row, c], acts.at[:, row, c], acts.at[:, row, 1 - c], pair_c)
        )

    def z_step(far):
        if far == 0:
            to_core(z)
        for way in DIRS:
            if far > Z_REACH[way]:
                continue
            row = mod(z - way * far, 8)
            if far > 0:
                z_copies[way, far - 1].arrived()
            if far < Z_REACH[way]:
                land = mod(z - way * (far + 1), 8)
                z_copies[way, far] = Copy(
                    acts.at[:, row, c], acts.at[:, row, c], acts.at[:, land, c], at_z(way)
                )
            if far > 0:
                to_core(row)

    def turned(value):
        return value.astype(F32).T.astype(BF16).reshape(16, rows, 128)

    z_step(0)
    y_step(1)
    z_step(1)
    y_step(2)
    z_step(2)
    y_step(3)
    z_step(3)
    y_step(4)
    z_step(4)
    for copy in c_copies:
        copy.arrived()
    xn[:, :, 0:128] = turned(acts[0].reshape(128, d))
    y_step(5)
    xn[:, :, 128:256] = turned(acts[1].reshape(128, d))
    y_step(6)
    xc[:, :, 0:128] = turned(acts[2].reshape(128, d))
    for way in DIRS:
        last = {sub: max(f for q, f in Y_ITEMS[way] if q == sub) for sub in (0, 1)}
        for sub in (0, 1):
            y_copies[way, sub, last[sub]].arrived()

    lane = lax.broadcasted_iota(jnp.int32, (128, 128), 1)

    def iterate(m, cot):
        normed = acts[m].reshape(128, d)

        def part(lo, hi):
            return w[:, :, :, lo:hi].reshape(d, hi - lo)

        def gate(hidden, back):
            sigma = jax.nn.sigmoid(hidden)
            return hidden * sigma, back * sigma * (1.0 + hidden * (1.0 - sigma))

        hidden_out, back_in = gate(dot(normed, part(0, 256)), dot(cot, part(256, 512)))
        rest = part(512, 640)
        rest_out, rest_in = gate(dot(normed, rest), pltpu.roll(dot(cot, rest), 96, 1))
        rest_out = jnp.where(lane < 32, rest_out, 0.0)
        rest_in = jnp.where(lane < 32, rest_in, 0.0)
        at_m = slice(128 * m, 128 * (m + 1))
        back_in = back_in.astype(BF16)
        rest_in = rest_in.astype(BF16)
        bm[at_m, :] = back_in
        br[at_m, :] = rest_in
        hm[at_m, :] = hidden_out.astype(BF16)
        hr[at_m, :] = pltpu.roll(rest_out, 32, 1).astype(BF16)
        term = []
        step = 896
        wide = part(0, 256)
        for k in range(0, d, step):
            partial = dot_t(back_in, wide[k : k + step]) + dot_t(rest_in, rest[k : k + step])
            pb[m, :, :, :, k : k + step] = partial.astype(BF16).reshape(8, 2, 8, step)
            term.append(
                jnp.sum(partial * normed[:, k : k + step].astype(F32), axis=0, keepdims=True)
            )
        return jnp.concatenate(term, axis=1)

    def sum_cores(m):
        return Copy(pb.at[m, :, 1 - c], rc.at[m], rc.at[m], pair_c)

    def sum_out(m, first):
        first.arrived()
        qb[m] = (pb[m, :, c].astype(F32) + rc[m].astype(F32)).astype(BF16)
        return [
            Copy(qb.at[m, mod(z + k, 8)], rz.at[m, k], rz.at[m, k], at_z(k)) for k in range(1, 8)
        ]

    def sum_in(m, parts):
        for copy in parts:
            copy.arrived()
        total = qb[m, z].astype(F32)
        for k in range(1, 8):
            total = total + rz[m, k].astype(F32)
        st[m] = total.astype(BF16)
        return Copy(st.at[m], sr.at[m], sr.at[m], pair_l)

    def sum_end(m, last, cot):
        last.arrived()
        gained = (st[m].astype(F32) + sr[m].astype(F32)) * gain_wide
        scaled, reciprocal = own_state(m)
        back_state = reciprocal * (
            gained - scaled * jnp.mean(gained * scaled, axis=-1, keepdims=True)
        )
        return (cot.astype(F32) + back_state).astype(BF16)

    gain_term = iterate(0, acts[2].reshape(128, d))
    last = sum_in(0, sum_out(0, sum_cores(0)))
    res[...] = sum_end(0, last, acts[2, z, c])
    hand = Copy(res, cots.at[z, c], cots.at[z, c], before)
    hand.arrived()

    def cots_to_core(row):
        return Copy(cots.at[row, c], cots.at[row, c], cots.at[row, 1 - c], pair_c)

    spread = [
        Copy(cots.at[z, c], cots.at[z, c], cots.at[mod(z - k, 8), c], at_z(k))
        for k in (4, 3, 5, 2, 6, 1, 7)
    ]
    across = [cots_to_core(z)]
    for k, copy in zip((4, 3, 5, 2, 6, 1, 7), spread):
        copy.arrived()
        across.append(cots_to_core(mod(z - k, 8)))
    for copy in across:
        copy.arrived()

    gain_term = gain_term + iterate(1, cots[...].reshape(128, d))
    first = sum_cores(1)
    ga[0] = gain_term * scale / gain_wide
    gain_c = Copy(ga.at[0], ga.at[1], ga.at[1], pair_c)
    xc[:, :, 128:256] = turned(cots[...].reshape(128, d))

    def terms(row, at_h):
        k = row * 2 + at_h
        left_n, left_c = xn[k], xc[k]
        return (
            dot(left_n, bm[...]) * scale,
            dot(left_c, hm[...]) * scale,
            (dot(left_n, br[...]) + dot(left_c, hr[...])) * scale,
        )

    LANES = ((0, 256), (256, 512), (512, 640))
    g_copies = {}

    def g_step(i):
        for way in DIRS:
            sub, far = G_ITEMS[way][i]
            value = terms(mod(y + way * far, 8), g if sub else h)
            n = 0 if way == 1 else 1
            if (way, sub, far + 1) in g_copies:
                k = G_ITEMS[way].index((sub, far + 1))
                g_copies[way, sub, far + 1].arrived()
                value = [t + gr[n, k, :, a:b].astype(F32) for t, (a, b) in zip(value, LANES)]
            for t, (a, b) in zip(value, LANES):
                gs[n, i, :, a:b] = t.astype(BF16)
            g_copies[way, sub, far] = Copy(gs.at[n, i], gr.at[n, i], gr.at[n, i], at_y(way))

    def g_end(sub):
        value = terms(y, g if sub else h)
        for n, way in enumerate(DIRS):
            g_copies[way, sub, 1].arrived()
            k = G_ITEMS[way].index((sub, 1))
            value = [t + gr[n, k, :, a:b].astype(F32) for t, (a, b) in zip(value, LANES)]
        return value

    g_step(0)
    parts = sum_out(1, first)
    g_step(1)
    gain_c.arrived()
    ga[2] = ga[0] + ga[1]
    gain_l = Copy(ga.at[2], ga.at[3], ga.at[3], pair_l)
    g_step(2)
    gain_l.arrived()
    ga[4] = ga[2] + ga[3]
    gain_h = Copy(ga.at[4], ga.at[5], ga.at[5], pair_h)
    last = sum_in(1, parts)
    g_step(3)
    gain_h.arrived()
    gz[z] = ga[4] + ga[5]
    gain_z = [Copy(gz.at[z], gz.at[z], gz.at[mod(z - k, 8)], at_z(k)) for k in range(1, 8)]
    result = sum_end(1, last, cots[z, c])
    cot_out[0] = jnp.where(l == 0, result[0:4].astype(F32), result[4:8].astype(F32)).astype(BF16)
    g_step(4)
    for copy in gain_z:
        copy.arrived()
    gy[y] = jnp.sum(gz[...], axis=0)
    gain_y = [Copy(gy.at[y], gy.at[y], gy.at[mod(y - k, 8)], at_y(k)) for k in range(1, 8)]
    g_step(5)
    for copy in gain_y:
        copy.arrived()
    gain_out[...] = jnp.sum(gy[...], axis=0)
    g_step(6)

    for t, (a, b) in zip(g_end(1), LANES):
        fs[:, a:b] = t.astype(BF16)
    final = Copy(fs, fr, fr, pair_h)
    up_main, down_main, rest = g_end(0)
    final.arrived()
    up_out[:, 0:256] = (up_main + fr[:, 0:256].astype(F32)).astype(BF16)
    rest = rest + fr[:, 512:640].astype(F32)
    up_out[:, 256:288] = rest[:, 0:32].astype(BF16)
    down_out[0:256, :] = (down_main + fr[:, 256:512].astype(F32)).T.astype(BF16)
    down_out[256:288, :] = rest.T[32:64, :].astype(BF16)

    assert count[0] == N_COPIES, count[0]
    for copy in pending:
        copy.out.wait_send()


N_COPIES = 98


def on_device(scale, saved_states, cotangent_in, lengths, gain, up_weight, down_weight):
    d = gain.shape[0]
    rows, cols = up_weight.shape
    vmem = pl.BlockSpec(memory_space=pltpu.VMEM)
    outs = pl.pallas_call(
        functools.partial(kernel, scale),
        out_shape=(
            jax.ShapeDtypeStruct((1, 4, d), BF16),
            jax.ShapeDtypeStruct((rows, cols), BF16),
            jax.ShapeDtypeStruct((cols, rows), BF16),
            jax.ShapeDtypeStruct((1, d), F32),
        ),
        in_specs=[vmem, vmem, pl.BlockSpec(memory_space=pltpu.SMEM), vmem, vmem, vmem],
        out_specs=(vmem,) * 4,
        scratch_shapes=[
            pltpu.VMEM((8, 2, rows, 640), BF16),
            pltpu.VMEM((2, 2, 4, d), BF16),
            pltpu.VMEM((2, 4, d), BF16),
            pltpu.VMEM((3, 8, 2, 8, d), BF16),
            pltpu.VMEM((8, 2, 8, d), BF16),
            pltpu.VMEM((16, rows, 256), BF16),
            pltpu.VMEM((16, rows, 256), BF16),
            pltpu.VMEM((256, 256), BF16),
            pltpu.VMEM((256, 256), BF16),
            pltpu.VMEM((256, 128), BF16),
            pltpu.VMEM((256, 128), BF16),
            pltpu.VMEM((2, 8, 2, 8, d), BF16),
            pltpu.VMEM((2, 8, 8, d), BF16),
            pltpu.VMEM((2, 8, 8, d), BF16),
            pltpu.VMEM((2, 8, 8, d), BF16),
            pltpu.VMEM((2, 8, d), BF16),
            pltpu.VMEM((2, 8, d), BF16),
            pltpu.VMEM((8, d), BF16),
            pltpu.VMEM((2, 7, rows, 640), BF16),
            pltpu.VMEM((2, 7, rows, 640), BF16),
            pltpu.VMEM((rows, 640), BF16),
            pltpu.VMEM((rows, 640), BF16),
            pltpu.VMEM((6, 1, d), F32),
            pltpu.VMEM((8, 1, d), F32),
            pltpu.VMEM((8, 1, d), F32),
            pltpu.SemaphoreType.DMA((N_COPIES,)),
            pltpu.SemaphoreType.DMA((N_COPIES,)),
        ],
        compiler_params=pltpu.CompilerParams(
            collective_id=0, has_side_effects=True, vmem_limit_bytes=56 * 2**20
        ),
    )(saved_states, cotangent_in, lengths, gain[None], up_weight, down_weight)
    return outs[0], outs[1], outs[2], outs[3][0]


def solution(mesh):
    placed = (
        P("section", None, "dp", None),
        P("section", "dp", None),
        P("section"),
        P(),
        P("section", "dp"),
        P("dp", "section"),
    )
    scale = 1.0 / math.sqrt(2 * 128 * mesh.shape["section"])
    return jax.shard_map(
        functools.partial(on_device, scale),
        mesh=mesh,
        in_specs=placed,
        out_specs=(P("section", "dp", None), P("section", "dp"), P("dp", "section"), P()),
        check_vma=False,
    )
```

```python
import functools
import math

import jax
import jax.numpy as jnp
from jax import lax
from jax.experimental import pallas as pl
from jax.experimental.pallas import tpu as pltpu
from jax.sharding import PartitionSpec as P

MESH = pl.DeviceIdType.MESH
F32, BF16 = jnp.float32, jnp.bfloat16
epsilon = 1e-06

A_ITEMS = {
    1: ((0, 0), (1, 0), (0, 1), (1, 1), (0, 2), (1, 2), (0, 3)),
    -1: ((0, 0), (1, 0), (0, 1), (1, 1), (0, 2), (1, 2), (1, 3)),
}
GA_ITEMS = {
    1: ((0, 4), (1, 3), (0, 3), (1, 2), (0, 2), (1, 1), (0, 1)),
    -1: ((1, 4), (0, 3), (1, 3), (0, 2), (1, 2), (0, 1), (1, 1)),
}
REACH = {1: 4, -1: 3}
DIRS = (1, -1)
N_COPIES = 160


def mod(a, n):
    return lax.rem(a + n, n)


def dot(a, b):
    return jnp.dot(a, b, preferred_element_type=F32)


def dot_t(a, b):
    return lax.dot_general(a, b, (((1,), (1,)), ((), ())), preferred_element_type=F32)


def b_pieces(way, far, last):
    return (0, 1) if far != last else (0,) if way == 1 else (1,)


def folded(rest):
    return jnp.concatenate([rest[0:80] + pltpu.roll(rest[88:168], 64, 1), rest[80:88]], axis=0)


def kernel(
    scale, states, cot_in, lengths, gain, up, down,
    cot_out, up_out, down_out, gain_out,
    wa, wb0, wb1, wr, e_s, e_c, n_s, n_c, nb, acts, cots, xn, xc, bm, hm, br, hr,
    pb, rc, qb, zs, rz, st, sr,
    gas, gar, gx0, gx1, hx0, hx1, gs0, gs1, gr0, gr1, fs, fr,
    ga, gz, gy, send, recv,
):
    s, p = lax.axis_index("section"), lax.axis_index("dp")
    y, h = lax.div(s, 2), lax.rem(s, 2)
    z, l, c = lax.div(p, 4), lax.rem(lax.div(p, 2), 2), lax.rem(p, 2)
    g = 1 - h
    wb, gx, hx, gs, gr = (wb0, wb1), (gx0, gx1), (hx0, hx1), (gs0, gs1), (gr0, gr1)

    def at(section=None, dp=None):
        return {"section": s if section is None else section, "dp": p if dp is None else dp}

    def at_y(k):
        return at(section=mod(y + k, 8) * 2 + h)

    def at_z(k):
        return at(dp=mod(z + k, 8) * 4 + l * 2 + c)

    other_l = p + 2 - 4 * l
    pair_h = at(section=s + 1 - 2 * h)
    pair_l = at(dp=other_l)
    pair_c = at(dp=p + 1 - 2 * c)
    before = at(section=mod(s - 1, 16))
    before_l = at(section=mod(s - 1, 16), dp=other_l)
    cross = mod(s - 1 + 2 * h, 16)

    pending = []

    class Copy:
        def __init__(self, src, dst, landing, device):
            k = len(pending)
            self.out = pltpu.make_async_remote_copy(
                src_ref=src, dst_ref=dst, send_sem=send.at[k], recv_sem=recv.at[k],
                device_id=device, device_id_type=MESH,
            )
            self.arrival = pltpu.make_async_remote_copy(
                src_ref=src, dst_ref=landing, send_sem=send.at[k], recv_sem=recv.at[k],
                device_id=device, device_id_type=MESH,
            )
            pending.append(self)
            self.out.start()

        def arrived(self):
            self.arrival.wait_recv()

    barrier = pltpu.get_barrier_semaphore()
    partners = [at_y(k) for k in range(1, 8)] + [at_z(k) for k in range(1, 8)]
    partners += [pair_h, pair_l, pair_c, at(section=cross)]
    partners += [at(section=s + 1 - 2 * h, dp=other_l), at(section=cross, dp=other_l)]
    for device in partners:
        pl.semaphore_signal(barrier, inc=1, device_id=device, device_id_type=MESH)

    rows = up.shape[0]
    wa[y, h] = up[:, 0:256]
    wb0[y, h, 0:rows, :] = down[:, 0:128]
    wb1[y, h] = down[:, 128:256]
    wb0[y, h, rows : rows + 88, :] = folded(
        jnp.concatenate(
            [up[:, 256:288].astype(F32), down[:, 256:288].astype(F32), jnp.zeros((rows, 64), F32)],
            axis=1,
        )
    ).astype(BF16)
    e_s[l] = states[0]
    e_c[l] = cot_in[0]

    pl.semaphore_wait(barrier, len(partners))

    swap_w = Copy(wa.at[y, h], wa.at[y, h], wa.at[y, g], pair_h)
    a_copies, b_copies, x_copies = {}, {}, []

    def a_step(i):
        for way in DIRS:
            sub, far = A_ITEMS[way][i]
            if far > 0:
                a_copies[way, sub, far - 1].arrived()
            elif sub == 1 and way == 1:
                swap_w.arrived()
            row = mod(y - way * far, 8)
            land = mod(y - way * (far + 1), 8)
            at_h = g if sub else h
            a_copies[way, sub, far] = Copy(wa.at[row, at_h], wa.at[row, at_h], wa.at[land, at_h], at_y(way))

    def b_across(row, j):
        x_copies.append(Copy(wb[j].at[row, h], wb[j].at[row, h], wb[j].at[row, g], pair_h))

    def b_step(far):
        for way in DIRS:
            row = mod(y - way * far, 8)
            land = mod(y - way * (far + 1), 8)
            for j in (0, 1):
                came = far > 0 and j in b_pieces(way, far - 1, 3)
                if came:
                    b_copies[way, j, far - 1].arrived()
                if far < 4 and j in b_pieces(way, far, 3):
                    b_copies[way, j, far] = Copy(
                        wb[j].at[row, h], wb[j].at[row, h], wb[j].at[land, h], at_y(way)
                    )
                if came:
                    b_across(row, j)

    b_step(0)
    a_step(0)
    swap_s = Copy(e_s.at[l], e_s.at[l], e_s.at[1 - l], pair_l)
    swap_c = Copy(e_c.at[l], e_c.at[l], e_c.at[1 - l], pair_l)
    a_step(1)
    b_across(y, 0)
    b_across(y, 1)

    d = gain.shape[0]
    gain_wide = gain[...].astype(F32).reshape(1, d)
    swap_s.arrived()
    swap_c.arrived()
    in_chunk = lax.broadcasted_iota(jnp.int32, (8, 1), 0)
    position = z * 16 + c * 4 + jnp.where(in_chunk >= 4, in_chunk + 4, in_chunk)

    def scaled_of(first, second):
        values = jnp.concatenate([first.astype(F32), second.astype(F32)], axis=0)
        reciprocal = lax.rsqrt(jnp.mean(values * values, axis=-1, keepdims=True) + epsilon)
        return values * reciprocal, reciprocal

    for m in range(2):
        acts[m, z, c] = (scaled_of(e_s[0, m], e_s[1, m])[0] * gain_wide).astype(BF16)
    raw = jnp.concatenate([e_c[0].astype(F32), e_c[1].astype(F32)], axis=0)
    acts[2, z, c] = jnp.where(position < lengths[0], raw, 0.0).astype(BF16)

    z_copies, c_copies = {}, []

    def ring_z(step, block, copies, to_core):
        for way in DIRS:
            if step > REACH[way]:
                continue
            row = mod(z - way * step, 8)
            if step > 0:
                copies[way, step - 1].arrived()
            if step < REACH[way]:
                land = mod(z - way * (step + 1), 8)
                copies[way, step] = Copy(block(row, c), block(row, c), block(land, c), at_z(way))
            if step > 0 or way == 1:
                to_core.append(Copy(block(row, c), block(row, c), block(row, 1 - c), pair_c))

    def z_step(step):
        ring_z(step, lambda row, core: acts.at[:, row, core], z_copies, c_copies)

    def turned(value):
        return value.astype(F32).T.astype(BF16).reshape(16, rows, 128)

    z_step(0)
    next_s = Copy(e_s.at[:, 0], n_s, n_s, before)
    next_c = Copy(acts.at[2, z, c], n_c, n_c, before)
    b_step(1)
    z_step(1)
    a_step(2)
    b_step(2)
    z_step(2)
    a_step(3)
    z_step(3)
    b_step(3)
    z_step(4)
    a_step(4)
    for copy in c_copies:
        copy.arrived()
    xn[:, :, 0:128] = turned(acts[0].reshape(128, d))
    b_step(4)
    a_step(5)
    xn[:, :, 128:256] = turned(acts[1].reshape(128, d))
    a_step(6)
    xc[:, :, 0:128] = turned(acts[2].reshape(128, d))
    next_s.arrived()
    next_c.arrived()
    for copy in x_copies:
        copy.arrived()
    for way in DIRS:
        for sub in (0, 1):
            last = max(f for q, f in A_ITEMS[way] if q == sub)
            a_copies[way, sub, last].arrived()
    for row in range(8):
        for k in range(2):
            fold = wb0[row, k, rows : rows + 88, :].astype(F32)
            wr[row, k] = jnp.concatenate([fold, pltpu.roll(fold[0:80], 64, 1)], axis=0).astype(BF16)

    lane = lax.broadcasted_iota(jnp.int32, (128, 128), 1)

    def gate(hidden, back):
        sigma = jax.nn.sigmoid(hidden)
        return hidden * sigma, back * sigma * (1.0 + hidden * (1.0 - sigma))

    def hidden_side(m, cot):
        normed = acts[m].reshape(128, d)
        down_main = jnp.concatenate(
            [wb0[:, :, 0:rows, :].reshape(d, 128), wb1[...].reshape(d, 128)], axis=1
        )
        hidden_out, back_in = gate(dot(normed, wa[...].reshape(d, 256)), dot(cot, down_main))
        rest = wr[...].reshape(d, 128)
        rest_out, rest_in = gate(dot(normed, rest), pltpu.roll(dot(cot, rest), 96, 1))
        rest_out = jnp.where(lane < 32, rest_out, 0.0)
        rest_in = jnp.where(lane < 32, rest_in, 0.0)
        at_m = slice(128 * m, 128 * (m + 1))
        bm[at_m, :] = back_in.astype(BF16)
        br[at_m, :] = rest_in.astype(BF16)
        hm[at_m, :] = hidden_out.astype(BF16)
        hr[at_m, :] = pltpu.roll(rest_out, 32, 1).astype(BF16)

    def back_side(m):
        normed = acts[m].reshape(128, d)
        at_m = slice(128 * m, 128 * (m + 1))
        back_in, rest_in = bm[at_m, :], br[at_m, :]
        wide, rest = wa[...].reshape(d, 256), wr[...].reshape(d, 128)
        term = []
        step = 896
        for k in range(0, d, step):
            partial = dot_t(back_in, wide[k : k + step]) + dot_t(rest_in, rest[k : k + step])
            pb[m, :, :, :, k : k + step] = partial.astype(BF16).reshape(8, 2, 8, step)
            term.append(
                jnp.sum(partial * normed[:, k : k + step].astype(F32), axis=0, keepdims=True)
            )
        return jnp.concatenate(term, axis=1), Copy(pb.at[m, :, 1 - c], rc.at[m], rc.at[m], pair_c)

    s_copies = {}

    def sum_step(m, step, first):
        if step == 0:
            first.arrived()
            qb[m] = (pb[m, :, c].astype(F32) + rc[m].astype(F32)).astype(BF16)
        for n, way in enumerate(DIRS):
            far = REACH[way] - step
            if far < 1:
                continue
            source = qb.at[m, mod(z + way * far, 8)]
            if step > 0:
                s_copies[m, way, step - 1].arrived()
                total = source[...].astype(F32) + rz[m, n, step - 1].astype(F32)
                source = zs.at[m, n, step]
                source[...] = total.astype(BF16)
            s_copies[m, way, step] = Copy(source, rz.at[m, n, step], rz.at[m, n, step], at_z(way))

    def sum_in(m):
        s_copies[m, 1, 3].arrived()
        s_copies[m, -1, 2].arrived()
        total = qb[m, z].astype(F32) + rz[m, 0, 3].astype(F32) + rz[m, 1, 2].astype(F32)
        st[m] = total.astype(BF16)

    def norm_side(back_normed, scaled, reciprocal, cot):
        gained = back_normed * gain_wide
        back_state = reciprocal * (
            gained - scaled * jnp.mean(gained * scaled, axis=-1, keepdims=True)
        )
        return (cot.astype(F32) + back_state).astype(BF16)

    hidden_side(0, acts[2].reshape(128, d))
    gain_term, first = back_side(0)
    for step in range(4):
        sum_step(0, step, first)
    scaled, reciprocal = scaled_of(n_s[0], n_s[1])
    sum_in(0)
    hands = [
        Copy(st.at[0], nb.at[l], nb.at[l], before),
        Copy(st.at[0], nb.at[l], nb.at[1 - l], before_l),
    ]
    for copy in hands:
        copy.arrived()
    cots[z, c] = norm_side(nb[0].astype(F32) + nb[1].astype(F32), scaled, reciprocal, n_c[...])
    r_copies, across = {}, []
    for step in range(5):
        ring_z(step, lambda row, core: cots.at[row, core], r_copies, across)
    for copy in across:
        copy.arrived()

    hidden_side(1, cots[...].reshape(128, d))
    ga_copies, gx_copies, gb_copies = {}, {}, {}

    def ga_step(i):
        for n, way in enumerate(DIRS):
            sub, far = GA_ITEMS[way][i]
            value = dot(xn[mod(y + way * far, 8) * 2 + (g if sub else h)], bm[...]) * scale
            if (way, sub, far + 1) in ga_copies:
                k = GA_ITEMS[way].index((sub, far + 1))
                ga_copies[way, sub, far + 1].arrived()
                value = value + gar[n, k].astype(F32)
            gas[n, i] = value.astype(BF16)
            ga_copies[way, sub, far] = Copy(gas.at[n, i], gar.at[n, i], gar.at[n, i], at_y(way))

    def ga_end(sub):
        value = dot(xn[y * 2 + (g if sub else h)], bm[...]) * scale
        for n, way in enumerate(DIRS):
            ga_copies[way, sub, 1].arrived()
            value = value + gar[n, GA_ITEMS[way].index((sub, 1))].astype(F32)
        return value

    def b_terms(far, at_h):
        k = mod(y + far, 8) * 2 + at_h
        left_n, left_c = xn[k], xc[k]
        main = dot(left_c, hm[...]) * scale
        rest = (dot(left_n, br[...]) + dot(left_c, hr[...])) * scale
        return [jnp.concatenate([main[:, 0:128], folded(rest)], axis=0), main[:, 128:256]]

    def gx_step(far):
        k = far + 3
        for j, value in enumerate(b_terms(far, g)):
            gx[j][k] = value.astype(BF16)
            gx_copies[far, j] = Copy(gx[j].at[k], hx[j].at[k], hx[j].at[k], pair_h)

    def b_pair(far):
        value = b_terms(far, h)
        for j in (0, 1):
            gx_copies[far, j].arrived()
            value[j] = value[j] + hx[j][far + 3].astype(F32)
        return value

    def gb_step(far):
        if far == 4:
            pair = b_pair(4)
        for n, way in enumerate(DIRS):
            if far < 4:
                pair = b_pair(way * far)
            for j in b_pieces(way, far, 4):
                value = pair[j]
                if (way, j, far + 1) in gb_copies:
                    gb_copies[way, j, far + 1].arrived()
                    value = value + gr[j][n, far + 1].astype(F32)
                gs[j][n, far] = value.astype(BF16)
                gb_copies[way, j, far] = Copy(
                    gs[j].at[n, far], gr[j].at[n, far], gr[j].at[n, far], at_y(way)
                )

    ga_step(0)
    ga_step(1)
    xc[:, :, 128:256] = turned(cots[...].reshape(128, d))
    gx_step(4)
    gx_step(3)
    gx_step(-3)
    term, first = back_side(1)
    ga[0] = (gain_term + term) * scale / gain_wide
    gain_c = Copy(ga.at[0], ga.at[1], ga.at[1], pair_c)
    ga_step(2)
    gx_step(2)
    gx_step(-2)
    gb_step(4)
    sum_step(1, 0, first)
    gx_step(1)
    gx_step(-1)
    gx_step(0)
    ga_step(3)
    sum_step(1, 1, first)
    gain_c.arrived()
    ga[2] = ga[0] + ga[1]
    gain_l = Copy(ga.at[2], ga.at[3], ga.at[3], pair_l)
    gb_step(3)
    sum_step(1, 2, first)
    gain_l.arrived()
    ga[4] = ga[2] + ga[3]
    gain_h = Copy(ga.at[4], ga.at[5], ga.at[5], pair_h)
    ga_step(4)
    sum_step(1, 3, first)
    gain_h.arrived()
    gz[z] = ga[4] + ga[5]
    gain_z = [Copy(gz.at[z], gz.at[z], gz.at[mod(z - k, 8)], at_z(k)) for k in range(1, 8)]
    gb_step(2)
    sum_in(1)
    last = Copy(st.at[1], sr, sr, pair_l)
    ga_step(5)
    for copy in gain_z:
        copy.arrived()
    gy[y] = jnp.sum(gz[...], axis=0)
    gain_y = [Copy(gy.at[y], gy.at[y], gy.at[mod(y - k, 8)], at_y(k)) for k in range(1, 8)]
    ga_step(6)
    gb_step(1)
    scaled, reciprocal = scaled_of(e_s[0, 1], e_s[1, 1])
    last.arrived()
    result = norm_side(st[1].astype(F32) + sr[...].astype(F32), scaled, reciprocal, cots[z, c])
    cot_out[0] = jnp.where(l == 0, result[0:4].astype(F32), result[4:8].astype(F32)).astype(BF16)
    for copy in gain_y:
        copy.arrived()
    gain_out[...] = jnp.sum(gy[...], axis=0).reshape(d)

    fs[...] = ga_end(1).astype(BF16)
    final = Copy(fs, fr, fr, pair_h)
    up_main = ga_end(0)
    down_main, fold = None, None
    pair = b_pair(0)
    for j in (0, 1):
        for n, way in enumerate(DIRS):
            gb_copies[way, j, 1].arrived()
            pair[j] = pair[j] + gr[j][n, 1].astype(F32)
    down_out[:, 0:128] = pair[0][0:rows].astype(BF16)
    down_out[:, 128:256] = pair[1].astype(BF16)
    fold = pair[0][rows : rows + 88]
    rest = jnp.concatenate([fold, pltpu.roll(fold[0:80], 64, 1)], axis=0)
    up_out[:, 256:288] = rest[:, 0:32].astype(BF16)
    down_out[:, 256:288] = rest[:, 32:64].astype(BF16)
    final.arrived()
    up_out[:, 0:256] = (up_main + fr[...].astype(F32)).astype(BF16)

    assert len(pending) == N_COPIES, len(pending)
    for copy in pending:
        copy.out.wait_send()


def on_device(scale, saved_states, cotangent_in, lengths, gain, up_weight, down_weight):
    d = gain.shape[0]
    rows, cols = up_weight.shape
    vmem = pl.BlockSpec(memory_space=pltpu.VMEM)
    scratch = dict(
        wa=(8, 2, rows, 256), wb0=(8, 2, rows + 88, 128), wb1=(8, 2, rows, 128), wr=(8, 2, rows, 128),
        e_s=(2, 2, 4, d), e_c=(2, 4, d), n_s=(2, 4, d), n_c=(8, d), nb=(2, 8, d),
        acts=(3, 8, 2, 8, d), cots=(8, 2, 8, d), xn=(16, rows, 256), xc=(16, rows, 256),
        bm=(256, 256), hm=(256, 256), br=(256, 128), hr=(256, 128),
        pb=(2, 8, 2, 8, d), rc=(2, 8, 8, d), qb=(2, 8, 8, d), zs=(2, 2, 4, 8, d), rz=(2, 2, 4, 8, d),
        st=(2, 8, d), sr=(8, d),
        gas=(2, 7, rows, 256), gar=(2, 7, rows, 256),
        gx0=(8, rows + 88, 128), gx1=(8, rows, 128), hx0=(8, rows + 88, 128), hx1=(8, rows, 128),
        gs0=(2, 5, rows + 88, 128), gs1=(2, 5, rows, 128),
        gr0=(2, 5, rows + 88, 128), gr1=(2, 5, rows, 128),
        fs=(rows, 256), fr=(rows, 256),
    )
    outs = pl.pallas_call(
        functools.partial(kernel, scale),
        out_shape=(
            jax.ShapeDtypeStruct((1, 4, d), BF16),
            jax.ShapeDtypeStruct((rows, cols), BF16),
            jax.ShapeDtypeStruct((rows, cols), BF16),
            jax.ShapeDtypeStruct((d,), F32),
        ),
        in_specs=[vmem, vmem, pl.BlockSpec(memory_space=pltpu.SMEM), vmem, vmem, vmem],
        out_specs=(vmem,) * 4,
        scratch_shapes=[pltpu.VMEM(shape, BF16) for shape in scratch.values()]
        + [pltpu.VMEM((n, 1, d), F32) for n in (6, 8, 8)]
        + [pltpu.SemaphoreType.DMA((N_COPIES,))] * 2,
        compiler_params=pltpu.CompilerParams(
            collective_id=0, has_side_effects=True, vmem_limit_bytes=56 * 2**20
        ),
    )(saved_states, cotangent_in, lengths, gain, up_weight, down_weight.T)
    return outs[0], outs[1], outs[2].T, outs[3]


def solution(mesh):
    placed = (
        P("section", None, "dp", None),
        P("section", "dp", None),
        P("section"),
        P(),
        P("section", "dp"),
        P("dp", "section"),
    )
    scale = 1.0 / math.sqrt(2 * 128 * mesh.shape["section"])
    return jax.shard_map(
        functools.partial(on_device, scale),
        mesh=mesh,
        in_specs=placed,
        out_specs=(P("section", "dp", None), P("section", "dp"), P("dp", "section"), P()),
        check_vma=False,
    )
```

```python
import functools
import math

import jax
import jax.numpy as jnp
from jax import lax
from jax.experimental import pallas as pl
from jax.experimental.pallas import tpu as pltpu
from jax.sharding import PartitionSpec as P

MESH = pl.DeviceIdType.MESH
F32, BF16 = jnp.float32, jnp.bfloat16
epsilon = 1e-06

A_ITEMS = {
    1: ((0, 0), (1, 0), (0, 1), (1, 1), (0, 2), (1, 2), (0, 3)),
    -1: ((0, 0), (1, 0), (0, 1), (1, 1), (0, 2), (1, 2), (1, 3)),
}
GA_ITEMS = {
    1: ((0, 4), (1, 3), (0, 3), (1, 2), (0, 2), (1, 1), (0, 1)),
    -1: ((1, 4), (0, 3), (1, 3), (0, 2), (1, 2), (0, 1), (1, 1)),
}
DIRS = (1, -1)
N_COPIES = 176


def mod(a, n):
    return lax.rem(a + n, n)


def dot(a, b):
    return jnp.dot(a, b, preferred_element_type=F32)


def dot_t(a, b):
    return lax.dot_general(a, b, (((1,), (1,)), ((), ())), preferred_element_type=F32)


def b_pieces(way, far, last):
    return (0, 1) if far != last else (0,) if way == 1 else (1,)


def folded(rest):
    return jnp.concatenate([rest[0:80] + pltpu.roll(rest[88:168], 64, 1), rest[80:88]], axis=0)


def kernel(
    scale, states, cot_in, lengths, gain, up, down,
    cot_out, up_out, down_out, gain_out,
    wa, wb0, wb1, wr, e_s, e_c, n_s, n_c, nb, acts, cots, xn, xc, bm, hm, br, hr,
    pb, rc, qb, rz, st, sr,
    gas, gar, gx0, gx1, hx0, hx1, gs0, gs1, gr0, gr1, fs, fr,
    ga, gz, gy, send, recv,
):
    s, p = lax.axis_index("section"), lax.axis_index("dp")
    y, h = lax.div(s, 2), lax.rem(s, 2)
    z, l, c = lax.div(p, 4), lax.rem(lax.div(p, 2), 2), lax.rem(p, 2)
    g = 1 - h
    wb, gx, hx, gs, gr = (wb0, wb1), (gx0, gx1), (hx0, hx1), (gs0, gs1), (gr0, gr1)

    def at(section=None, dp=None):
        return {"section": s if section is None else section, "dp": p if dp is None else dp}

    def at_y(k):
        return at(section=mod(y + k, 8) * 2 + h)

    def at_z(k):
        return at(dp=mod(z + k, 8) * 4 + l * 2 + c)

    other_l = p + 2 - 4 * l
    pair_h = at(section=s + 1 - 2 * h)
    pair_l = at(dp=other_l)
    pair_c = at(dp=p + 1 - 2 * c)
    pair_hl = at(section=s + 1 - 2 * h, dp=other_l)
    before = at(section=mod(s - 1, 16))
    before_l = at(section=mod(s - 1, 16), dp=other_l)
    cross = mod(s - 1 + 2 * h, 16)

    pending = []

    class Copy:
        def __init__(self, src, dst, landing, device):
            k = len(pending)
            self.out = pltpu.make_async_remote_copy(
                src_ref=src, dst_ref=dst, send_sem=send.at[k], recv_sem=recv.at[k],
                device_id=device, device_id_type=MESH,
            )
            self.arrival = pltpu.make_async_remote_copy(
                src_ref=src, dst_ref=landing, send_sem=send.at[k], recv_sem=recv.at[k],
                device_id=device, device_id_type=MESH,
            )
            pending.append(self)
            self.out.start()

        def arrived(self):
            self.arrival.wait_recv()

    barrier = pltpu.get_barrier_semaphore()
    partners = [at_y(k) for k in range(1, 8)] + [at_z(k) for k in range(1, 8)]
    partners += [pair_h, pair_l, pair_c, at(section=cross)]
    partners += [pair_hl, at(section=cross, dp=other_l)]
    for device in partners:
        pl.semaphore_signal(barrier, inc=1, device_id=device, device_id_type=MESH)

    rows = up.shape[0]
    wa[y, h] = up[:, 0:256]
    wb0[y, h, 0:rows, :] = down[:, 0:128]
    wb1[y, h] = down[:, 128:256]
    wb0[y, h, rows : rows + 88, :] = folded(
        jnp.concatenate(
            [up[:, 256:288].astype(F32), down[:, 256:288].astype(F32), jnp.zeros((rows, 64), F32)],
            axis=1,
        )
    ).astype(BF16)
    e_s[l] = states[0]
    e_c[l] = cot_in[0]

    pl.semaphore_wait(barrier, len(partners))

    swap_s = Copy(e_s.at[l], e_s.at[l], e_s.at[1 - l], pair_l)
    swap_c = Copy(e_c.at[l], e_c.at[l], e_c.at[1 - l], pair_l)
    swap_w = Copy(wa.at[y, h], wa.at[y, h], wa.at[y, g], pair_h)
    a_copies, b_copies, x_copies = {}, {}, []

    def a_step(i):
        for way in DIRS:
            sub, far = A_ITEMS[way][i]
            if far > 0:
                a_copies[way, sub, far - 1].arrived()
            elif sub == 1 and way == 1:
                swap_w.arrived()
            row = mod(y - way * far, 8)
            land = mod(y - way * (far + 1), 8)
            at_h = g if sub else h
            a_copies[way, sub, far] = Copy(wa.at[row, at_h], wa.at[row, at_h], wa.at[land, at_h], at_y(way))

    def b_across(row, j):
        x_copies.append(Copy(wb[j].at[row, h], wb[j].at[row, h], wb[j].at[row, g], pair_h))

    def b_step(far):
        for way in DIRS:
            row = mod(y - way * far, 8)
            land = mod(y - way * (far + 1), 8)
            for j in (0, 1):
                came = far > 0 and j in b_pieces(way, far - 1, 3)
                if came:
                    b_copies[way, j, far - 1].arrived()
                if far < 4 and j in b_pieces(way, far, 3):
                    b_copies[way, j, far] = Copy(
                        wb[j].at[row, h], wb[j].at[row, h], wb[j].at[land, h], at_y(way)
                    )
                if came:
                    b_across(row, j)

    b_step(0)
    a_step(0)
    b_across(y, 0)
    b_across(y, 1)
    b_step(1)

    d = gain.shape[0]
    gain_wide = gain[...].astype(F32).reshape(1, d)
    swap_s.arrived()
    swap_c.arrived()
    in_chunk = lax.broadcasted_iota(jnp.int32, (8, 1), 0)
    position = z * 16 + c * 4 + jnp.where(in_chunk >= 4, in_chunk + 4, in_chunk)

    def scaled_of(first, second):
        values = jnp.concatenate([first.astype(F32), second.astype(F32)], axis=0)
        reciprocal = lax.rsqrt(jnp.mean(values * values, axis=-1, keepdims=True) + epsilon)
        return values * reciprocal, reciprocal

    for m in range(2):
        acts[2 * m, z, c] = (scaled_of(e_s[0, m], e_s[1, m])[0] * gain_wide).astype(BF16)
    raw = jnp.concatenate([e_c[0].astype(F32), e_c[1].astype(F32)], axis=0)
    acts[1, z, c] = jnp.where(position < lengths[0], raw, 0.0).astype(BF16)

    FIRST, SECOND = slice(0, 2), slice(2, 3)
    z_copies, c_copies = {}, []

    def act(part, row, core):
        return acts.at[part, row, core]

    def z_send(part, k, row, far):
        row, land = mod(row, 8), mod(z - far, 8)
        z_copies[part.start, far] = Copy(act(part, row, c), act(part, row, c), act(part, land, c), at_z(k))

    def z_core(part, row):
        row = mod(row, 8)
        c_copies.append(Copy(act(part, row, c), act(part, row, c), act(part, row, 1 - c), pair_c))

    def z_near(part):
        for k in (2, -2, 1, -1):
            z_send(part, k, z, k)
        z_core(part, z)

    def z_far(part):
        z_copies[part.start, 2].arrived()
        z_send(part, 2, z - 2, 4)
        z_send(part, 1, z - 2, 3)
        z_copies[part.start, -2].arrived()
        z_send(part, -1, z + 2, -3)
        for k in (2, -2, 1, -1):
            if k in (1, -1):
                z_copies[part.start, k].arrived()
            z_core(part, z - k)

    def z_last(part):
        for k in (3, -3, 4):
            z_copies[part.start, k].arrived()
            z_core(part, z - k)

    def turned(value):
        return value.astype(F32).T.astype(BF16).reshape(16, rows, 128)

    z_near(FIRST)
    z_near(SECOND)
    a_step(2)
    a_step(1)
    next_s = Copy(e_s.at[:, 0], n_s, n_s, before)
    next_c = Copy(acts.at[1, z, c], n_c, n_c, before)
    b_step(2)
    a_step(4)
    z_far(FIRST)
    a_step(3)
    b_step(3)
    a_step(5)
    z_far(SECOND)
    b_step(4)
    a_step(6)
    z_last(FIRST)
    z_last(SECOND)
    for copy in c_copies:
        copy.arrived()
    xn[:, :, 0:128] = turned(acts[0].reshape(128, d))
    xn[:, :, 128:256] = turned(acts[2].reshape(128, d))
    xc[:, :, 0:128] = turned(acts[1].reshape(128, d))
    next_s.arrived()
    next_c.arrived()
    for way in DIRS:
        for sub in (0, 1):
            last = max(f for q, f in A_ITEMS[way] if q == sub)
            a_copies[way, sub, last].arrived()
    for copy in x_copies:
        copy.arrived()
    for row in range(8):
        for k in range(2):
            fold = wb0[row, k, rows : rows + 88, :].astype(F32)
            wr[row, k] = jnp.concatenate([fold, pltpu.roll(fold[0:80], 64, 1)], axis=0).astype(BF16)

    lane = lax.broadcasted_iota(jnp.int32, (128, 128), 1)

    def gate(hidden, back):
        sigma = jax.nn.sigmoid(hidden)
        return hidden * sigma, back * sigma * (1.0 + hidden * (1.0 - sigma))

    def hidden_side(m, cot):
        normed = acts[2 * m].reshape(128, d)
        down_main = jnp.concatenate(
            [wb0[:, :, 0:rows, :].reshape(d, 128), wb1[...].reshape(d, 128)], axis=1
        )
        hidden_out, back_in = gate(dot(normed, wa[...].reshape(d, 256)), dot(cot, down_main))
        rest = wr[...].reshape(d, 128)
        rest_out, rest_in = gate(dot(normed, rest), pltpu.roll(dot(cot, rest), 96, 1))
        rest_out = jnp.where(lane < 32, rest_out, 0.0)
        rest_in = jnp.where(lane < 32, rest_in, 0.0)
        at_m = slice(128 * m, 128 * (m + 1))
        bm[at_m, :] = back_in.astype(BF16)
        br[at_m, :] = rest_in.astype(BF16)
        hm[at_m, :] = hidden_out.astype(BF16)
        hr[at_m, :] = pltpu.roll(rest_out, 32, 1).astype(BF16)

    def back_side(m):
        normed = acts[2 * m].reshape(128, d)
        at_m = slice(128 * m, 128 * (m + 1))
        back_in, rest_in = bm[at_m, :], br[at_m, :]
        wide, rest = wa[...].reshape(d, 256), wr[...].reshape(d, 128)
        term = []
        step = 896
        for k in range(0, d, step):
            partial = dot_t(back_in, wide[k : k + step]) + dot_t(rest_in, rest[k : k + step])
            pb[m, :, :, :, k : k + step] = partial.astype(BF16).reshape(8, 2, 8, step)
            term.append(
                jnp.sum(partial * normed[:, k : k + step].astype(F32), axis=0, keepdims=True)
            )
        return jnp.concatenate(term, axis=1), Copy(pb.at[m, :, 1 - c], rc.at[m], rc.at[m], pair_c)

    FARTHEST_FIRST = (4, 3, 5, 2, 6, 1, 7)

    def sum_out(m, first):
        first.arrived()
        qb[m] = (pb[m, :, c].astype(F32) + rc[m].astype(F32)).astype(BF16)
        return [
            Copy(qb.at[m, mod(z + k, 8)], rz.at[m, k], rz.at[m, k], at_z(k)) for k in FARTHEST_FIRST
        ]

    def sum_in(m, parts):
        total = qb[m, z].astype(F32)
        for k, copy in zip(FARTHEST_FIRST, parts):
            copy.arrived()
            total = total + rz[m, k].astype(F32)
        st[m] = total.astype(BF16)

    def norm_side(back_normed, scaled, reciprocal, cot):
        gained = back_normed * gain_wide
        back_state = reciprocal * (
            gained - scaled * jnp.mean(gained * scaled, axis=-1, keepdims=True)
        )
        return (cot.astype(F32) + back_state).astype(BF16)

    hidden_side(0, acts[1].reshape(128, d))
    gain_term, first = back_side(0)
    parts = sum_out(0, first)
    scaled, reciprocal = scaled_of(n_s[0], n_s[1])
    sum_in(0, parts)
    hands = [
        Copy(st.at[0], nb.at[l], nb.at[l], before),
        Copy(st.at[0], nb.at[l], nb.at[1 - l], before_l),
    ]
    for copy in hands:
        copy.arrived()
    cots[z, c] = norm_side(nb[0].astype(F32) + nb[1].astype(F32), scaled, reciprocal, n_c[...])

    def cots_to_core(row):
        return Copy(cots.at[row, c], cots.at[row, c], cots.at[row, 1 - c], pair_c)

    spread = [
        Copy(cots.at[z, c], cots.at[z, c], cots.at[mod(z - k, 8), c], at_z(k)) for k in FARTHEST_FIRST
    ]
    across = [cots_to_core(z)]
    for k, copy in zip(FARTHEST_FIRST, spread):
        copy.arrived()
        across.append(cots_to_core(mod(z - k, 8)))
    for copy in across:
        copy.arrived()

    hidden_side(1, cots[...].reshape(128, d))
    ga_copies, gx_copies, gb_copies = {}, {}, {}

    def ga_step(i):
        for n, way in enumerate(DIRS):
            sub, far = GA_ITEMS[way][i]
            value = dot(xn[mod(y + way * far, 8) * 2 + (g if sub else h)], bm[...]) * scale
            if (way, sub, far + 1) in ga_copies:
                k = GA_ITEMS[way].index((sub, far + 1))
                ga_copies[way, sub, far + 1].arrived()
                value = value + gar[n, k].astype(F32)
            gas[n, i] = value.astype(BF16)
            ga_copies[way, sub, far] = Copy(gas.at[n, i], gar.at[n, i], gar.at[n, i], at_y(way))

    def ga_end(sub):
        value = dot(xn[y * 2 + (g if sub else h)], bm[...]) * scale
        for n, way in enumerate(DIRS):
            ga_copies[way, sub, 1].arrived()
            value = value + gar[n, GA_ITEMS[way].index((sub, 1))].astype(F32)
        return value

    def b_terms(far, at_h):
        k = mod(y + far, 8) * 2 + at_h
        left_n, left_c = xn[k], xc[k]
        main = dot(left_c, hm[...]) * scale
        rest = (dot(left_n, br[...]) + dot(left_c, hr[...])) * scale
        return [jnp.concatenate([main[:, 0:128], folded(rest)], axis=0), main[:, 128:256]]

    def gx_step(far):
        k = far + 3
        for j, value in enumerate(b_terms(far, g)):
            gx[j][k] = value.astype(BF16)
            gx_copies[far, j] = Copy(gx[j].at[k], hx[j].at[k], hx[j].at[k], pair_h)

    def b_pair(far):
        value = b_terms(far, h)
        for j in (0, 1):
            gx_copies[far, j].arrived()
            value[j] = value[j] + hx[j][far + 3].astype(F32)
        return value

    def gb_step(far):
        if far == 4:
            pair = b_pair(4)
        for n, way in enumerate(DIRS):
            if far < 4:
                pair = b_pair(way * far)
            for j in b_pieces(way, far, 4):
                value = pair[j]
                if (way, j, far + 1) in gb_copies:
                    gb_copies[way, j, far + 1].arrived()
                    value = value + gr[j][n, far + 1].astype(F32)
                gs[j][n, far] = value.astype(BF16)
                gb_copies[way, j, far] = Copy(
                    gs[j].at[n, far], gr[j].at[n, far], gr[j].at[n, far], at_y(way)
                )

    ga_step(0)
    ga_step(1)
    xc[:, :, 128:256] = turned(cots[...].reshape(128, d))
    for far in (4, 3, -3, 2, -2):
        gx_step(far)
    ga_step(2)
    term, first = back_side(1)
    ga[0] = (gain_term + term) * scale / gain_wide
    gain_c = Copy(ga.at[0], ga.at[1], ga.at[1], pair_c)
    for far in (1, -1, 0):
        gx_step(far)
    ga_step(3)
    parts = sum_out(1, first)
    gain_c.arrived()
    ga[2 + 2 * h + l] = ga[0] + ga[1]
    mine = ga.at[2 + 2 * h + l]
    gain_x = [
        Copy(mine, mine, ga.at[2 + 2 * h + 1 - l], pair_l),
        Copy(mine, mine, ga.at[2 + 2 * g + l], pair_h),
        Copy(mine, mine, ga.at[2 + 2 * g + 1 - l], pair_hl),
    ]
    gb_step(4)
    ga_step(4)
    for copy in gain_x:
        copy.arrived()
    gz[z] = (ga[2] + ga[3]) + (ga[4] + ga[5])
    gain_z = [Copy(gz.at[z], gz.at[z], gz.at[mod(z - k, 8)], at_z(k)) for k in FARTHEST_FIRST]
    gb_step(3)
    ga_step(5)
    for copy in gain_z:
        copy.arrived()
    gy[y] = jnp.sum(gz[...], axis=0)
    gain_y = [Copy(gy.at[y], gy.at[y], gy.at[mod(y - k, 8)], at_y(k)) for k in FARTHEST_FIRST]
    ga_step(6)
    sum_in(1, parts)
    last = Copy(st.at[1], sr, sr, pair_l)
    gb_step(2)
    fs[...] = ga_end(1).astype(BF16)
    final = Copy(fs, fr, fr, pair_h)
    gb_step(1)
    scaled, reciprocal = scaled_of(e_s[0, 1], e_s[1, 1])
    last.arrived()
    result = norm_side(st[1].astype(F32) + sr[...].astype(F32), scaled, reciprocal, cots[z, c])
    cot_out[0] = jnp.where(l == 0, result[0:4].astype(F32), result[4:8].astype(F32)).astype(BF16)
    for copy in gain_y:
        copy.arrived()
    gain_out[...] = jnp.sum(gy[...], axis=0).reshape(d)
    up_main = ga_end(0)
    pair = b_pair(0)
    for j in (0, 1):
        for n, way in enumerate(DIRS):
            gb_copies[way, j, 1].arrived()
            pair[j] = pair[j] + gr[j][n, 1].astype(F32)
    down_out[:, 0:128] = pair[0][0:rows].astype(BF16)
    down_out[:, 128:256] = pair[1].astype(BF16)
    fold = pair[0][rows : rows + 88]
    rest = jnp.concatenate([fold, pltpu.roll(fold[0:80], 64, 1)], axis=0)
    up_out[:, 256:288] = rest[:, 0:32].astype(BF16)
    down_out[:, 256:288] = rest[:, 32:64].astype(BF16)
    final.arrived()
    up_out[:, 0:256] = (up_main + fr[...].astype(F32)).astype(BF16)

    assert len(pending) == N_COPIES, len(pending)
    for copy in pending:
        copy.out.wait_send()


def on_device(scale, saved_states, cotangent_in, lengths, gain, up_weight, down_weight):
    d = gain.shape[0]
    rows, cols = up_weight.shape
    vmem = pl.BlockSpec(memory_space=pltpu.VMEM)
    scratch = dict(
        wa=(8, 2, rows, 256), wb0=(8, 2, rows + 88, 128), wb1=(8, 2, rows, 128), wr=(8, 2, rows, 128),
        e_s=(2, 2, 4, d), e_c=(2, 4, d), n_s=(2, 4, d), n_c=(8, d), nb=(2, 8, d),
        acts=(3, 8, 2, 8, d), cots=(8, 2, 8, d), xn=(16, rows, 256), xc=(16, rows, 256),
        bm=(256, 256), hm=(256, 256), br=(256, 128), hr=(256, 128),
        pb=(2, 8, 2, 8, d), rc=(2, 8, 8, d), qb=(2, 8, 8, d), rz=(2, 8, 8, d),
        st=(2, 8, d), sr=(8, d),
        gas=(2, 7, rows, 256), gar=(2, 7, rows, 256),
        gx0=(8, rows + 88, 128), gx1=(8, rows, 128), hx0=(8, rows + 88, 128), hx1=(8, rows, 128),
        gs0=(2, 5, rows + 88, 128), gs1=(2, 5, rows, 128),
        gr0=(2, 5, rows + 88, 128), gr1=(2, 5, rows, 128),
        fs=(rows, 256), fr=(rows, 256),
    )
    outs = pl.pallas_call(
        functools.partial(kernel, scale),
        out_shape=(
            jax.ShapeDtypeStruct((1, 4, d), BF16),
            jax.ShapeDtypeStruct((rows, cols), BF16),
            jax.ShapeDtypeStruct((rows, cols), BF16),
            jax.ShapeDtypeStruct((d,), F32),
        ),
        in_specs=[vmem, vmem, pl.BlockSpec(memory_space=pltpu.SMEM), vmem, vmem, vmem],
        out_specs=(vmem,) * 4,
        scratch_shapes=[pltpu.VMEM(shape, BF16) for shape in scratch.values()]
        + [pltpu.VMEM((n, 1, d), F32) for n in (6, 8, 8)]
        + [pltpu.SemaphoreType.DMA((N_COPIES,))] * 2,
        compiler_params=pltpu.CompilerParams(
            collective_id=0, has_side_effects=True, vmem_limit_bytes=56 * 2**20
        ),
    )(saved_states, cotangent_in, lengths, gain, up_weight, down_weight.T)
    return outs[0], outs[1], outs[2].T, outs[3]


def solution(mesh):
    placed = (
        P("section", None, "dp", None),
        P("section", "dp", None),
        P("section"),
        P(),
        P("section", "dp"),
        P("dp", "section"),
    )
    scale = 1.0 / math.sqrt(2 * 128 * mesh.shape["section"])
    return jax.shard_map(
        functools.partial(on_device, scale),
        mesh=mesh,
        in_specs=placed,
        out_specs=(P("section", "dp", None), P("section", "dp"), P("dp", "section"), P()),
        check_vma=False,
    )
```

```python
import functools
import math

import jax
import jax.numpy as jnp
from jax import lax
from jax.experimental import pallas as pl
from jax.experimental.pallas import tpu as pltpu
from jax.sharding import PartitionSpec as P

MESH = pl.DeviceIdType.MESH
F32, BF16 = jnp.float32, jnp.bfloat16
epsilon = 1e-06

A_ITEMS = {
    1: ((0, 0), (1, 0), (0, 1), (1, 1), (0, 2), (1, 2), (0, 3)),
    -1: ((0, 0), (1, 0), (0, 1), (1, 1), (0, 2), (1, 2), (1, 3)),
}
GA_ITEMS = {
    1: ((0, 4), (1, 3), (0, 3), (1, 2), (0, 2), (1, 1), (0, 1)),
    -1: ((1, 4), (0, 3), (1, 3), (0, 2), (1, 2), (0, 1), (1, 1)),
}
DIRS = (1, -1)
N_COPIES = 176


def mod(a, n):
    return lax.rem(a + n, n)


def dot(a, b):
    return jnp.dot(a, b, preferred_element_type=F32)


def dot_t(a, b):
    return lax.dot_general(a, b, (((1,), (1,)), ((), ())), preferred_element_type=F32)


def b_pieces(way, far, last):
    return (0, 1) if far != last else (0,) if way == 1 else (1,)


def folded(rest):
    return jnp.concatenate([rest[0:80] + pltpu.roll(rest[88:168], 64, 1), rest[80:88]], axis=0)


def kernel(
    scale, states, cot_in, lengths, gain, up, down,
    cot_out, up_out, down_out, gain_out,
    wa, wb0, wb1, wr, e_s, e_c, n_s, n_c, nb, acts, cots, xn, xc, bm, hm, br, hr,
    pb, rc, qb, rz, st, sr,
    gas, gar, gx0, gx1, hx0, hx1, gs0, gs1, gr0, gr1, fs, fr,
    ga, gz, gy, send, recv,
):
    s, p = lax.axis_index("section"), lax.axis_index("dp")
    y, h = lax.div(s, 2), lax.rem(s, 2)
    z, l, c = lax.div(p, 4), lax.rem(lax.div(p, 2), 2), lax.rem(p, 2)
    g = 1 - h
    wb, gx, hx, gs, gr = (wb0, wb1), (gx0, gx1), (hx0, hx1), (gs0, gs1), (gr0, gr1)

    def at(section=None, dp=None):
        return {"section": s if section is None else section, "dp": p if dp is None else dp}

    def at_y(k):
        return at(section=mod(y + k, 8) * 2 + h)

    def at_z(k):
        return at(dp=mod(z + k, 8) * 4 + l * 2 + c)

    other_l = p + 2 - 4 * l
    pair_h = at(section=s + 1 - 2 * h)
    pair_l = at(dp=other_l)
    pair_c = at(dp=p + 1 - 2 * c)
    pair_hl = at(section=s + 1 - 2 * h, dp=other_l)
    before = at(section=mod(s - 1, 16))
    before_l = at(section=mod(s - 1, 16), dp=other_l)
    cross = mod(s - 1 + 2 * h, 16)

    pending = []

    class Copy:
        def __init__(self, src, dst, landing, device):
            k = len(pending)
            self.out = pltpu.make_async_remote_copy(
                src_ref=src, dst_ref=dst, send_sem=send.at[k], recv_sem=recv.at[k],
                device_id=device, device_id_type=MESH,
            )
            self.arrival = pltpu.make_async_remote_copy(
                src_ref=src, dst_ref=landing, send_sem=send.at[k], recv_sem=recv.at[k],
                device_id=device, device_id_type=MESH,
            )
            pending.append(self)
            self.out.start()

        def arrived(self):
            self.arrival.wait_recv()

    barrier = pltpu.get_barrier_semaphore()
    partners = [at_y(k) for k in range(1, 8)] + [at_z(k) for k in range(1, 8)]
    partners += [pair_h, pair_l, pair_c, at(section=cross)]
    partners += [pair_hl, at(section=cross, dp=other_l)]
    for device in partners:
        pl.semaphore_signal(barrier, inc=1, device_id=device, device_id_type=MESH)

    rows = up.shape[0]
    wa[y, h] = up[:, 0:256]
    wb0[y, h, 0:rows, :] = down[:, 0:128]
    wb1[y, h] = down[:, 128:256]
    wb0[y, h, rows : rows + 88, :] = folded(
        jnp.concatenate(
            [up[:, 256:288].astype(F32), down[:, 256:288].astype(F32), jnp.zeros((rows, 64), F32)],
            axis=1,
        )
    ).astype(BF16)
    e_s[l] = states[0]
    e_c[l] = cot_in[0]

    pl.semaphore_wait(barrier, len(partners))

    swap_s = Copy(e_s.at[l], e_s.at[l], e_s.at[1 - l], pair_l)
    swap_c = Copy(e_c.at[l], e_c.at[l], e_c.at[1 - l], pair_l)
    swap_w = Copy(wa.at[y, h], wa.at[y, h], wa.at[y, g], pair_h)
    a_copies, b_copies, x_copies = {}, {}, []

    def a_step(i):
        for way in DIRS:
            sub, far = A_ITEMS[way][i]
            if far > 0:
                a_copies[way, sub, far - 1].arrived()
            elif sub == 1 and way == 1:
                swap_w.arrived()
            row = mod(y - way * far, 8)
            land = mod(y - way * (far + 1), 8)
            at_h = g if sub else h
            a_copies[way, sub, far] = Copy(wa.at[row, at_h], wa.at[row, at_h], wa.at[land, at_h], at_y(way))

    def b_across(row, j):
        x_copies.append(Copy(wb[j].at[row, h], wb[j].at[row, h], wb[j].at[row, g], pair_h))

    def b_step(far):
        for way in DIRS:
            row = mod(y - way * far, 8)
            land = mod(y - way * (far + 1), 8)
            for j in (0, 1):
                came = far > 0 and j in b_pieces(way, far - 1, 3)
                if came:
                    b_copies[way, j, far - 1].arrived()
                if far < 4 and j in b_pieces(way, far, 3):
                    b_copies[way, j, far] = Copy(
                        wb[j].at[row, h], wb[j].at[row, h], wb[j].at[land, h], at_y(way)
                    )
                if came:
                    b_across(row, j)

    b_step(0)
    a_step(0)
    b_across(y, 0)
    b_across(y, 1)
    b_step(1)

    d = gain.shape[0]
    gain_wide = gain[...].astype(F32).reshape(1, d)
    swap_s.arrived()
    swap_c.arrived()
    in_chunk = lax.broadcasted_iota(jnp.int32, (8, 1), 0)
    position = z * 16 + c * 4 + jnp.where(in_chunk >= 4, in_chunk + 4, in_chunk)

    def scaled_of(first, second):
        values = jnp.concatenate([first.astype(F32), second.astype(F32)], axis=0)
        reciprocal = lax.rsqrt(jnp.mean(values * values, axis=-1, keepdims=True) + epsilon)
        return values * reciprocal, reciprocal

    for m in range(2):
        acts[2 * m, z, c] = (scaled_of(e_s[0, m], e_s[1, m])[0] * gain_wide).astype(BF16)
    raw = jnp.concatenate([e_c[0].astype(F32), e_c[1].astype(F32)], axis=0)
    acts[1, z, c] = jnp.where(position < lengths[0], raw, 0.0).astype(BF16)

    FIRST, SECOND = slice(0, 2), slice(2, 3)
    z_copies, c_copies = {}, []

    def act(part, row, core):
        return acts.at[part, row, core]

    def z_send(part, k, row, far):
        row, land = mod(row, 8), mod(z - far, 8)
        z_copies[part.start, far] = Copy(act(part, row, c), act(part, row, c), act(part, land, c), at_z(k))

    def z_core(part, row):
        row = mod(row, 8)
        c_copies.append(Copy(act(part, row, c), act(part, row, c), act(part, row, 1 - c), pair_c))

    def z_near(part):
        for k in (2, -2, 1, -1):
            z_send(part, k, z, k)
        z_core(part, z)

    def z_far(part):
        z_copies[part.start, 2].arrived()
        z_send(part, 2, z - 2, 4)
        z_send(part, 1, z - 2, 3)
        z_copies[part.start, -2].arrived()
        z_send(part, -1, z + 2, -3)
        for k in (2, -2, 1, -1):
            if k in (1, -1):
                z_copies[part.start, k].arrived()
            z_core(part, z - k)

    def z_last(part):
        for k in (3, -3, 4):
            z_copies[part.start, k].arrived()
            z_core(part, z - k)

    def turned(value):
        return value.astype(F32).T.astype(BF16).reshape(16, rows, 128)

    z_near(FIRST)
    a_step(1)
    z_near(SECOND)
    a_step(2)
    next_s = Copy(e_s.at[:, 0], n_s, n_s, before)
    next_c = Copy(acts.at[1, z, c], n_c, n_c, before)
    b_step(2)
    a_step(3)
    z_far(FIRST)
    a_step(4)
    b_step(3)
    a_step(5)
    z_far(SECOND)
    b_step(4)
    a_step(6)
    z_last(FIRST)
    z_last(SECOND)
    for copy in c_copies:
        copy.arrived()
    xn[:, :, 0:128] = turned(acts[0].reshape(128, d))
    xn[:, :, 128:256] = turned(acts[2].reshape(128, d))
    xc[:, :, 0:128] = turned(acts[1].reshape(128, d))
    next_s.arrived()
    next_c.arrived()
    for way in DIRS:
        for sub in (0, 1):
            last = max(f for q, f in A_ITEMS[way] if q == sub)
            a_copies[way, sub, last].arrived()
    for copy in x_copies:
        copy.arrived()
    for row in range(8):
        for k in range(2):
            fold = wb0[row, k, rows : rows + 88, :].astype(F32)
            wr[row, k] = jnp.concatenate([fold, pltpu.roll(fold[0:80], 64, 1)], axis=0).astype(BF16)

    lane = lax.broadcasted_iota(jnp.int32, (128, 128), 1)

    def gate(hidden, back):
        sigma = jax.nn.sigmoid(hidden)
        return hidden * sigma, back * sigma * (1.0 + hidden * (1.0 - sigma))

    def hidden_side(m, cot):
        normed = acts[2 * m].reshape(128, d)
        down_main = jnp.concatenate(
            [wb0[:, :, 0:rows, :].reshape(d, 128), wb1[...].reshape(d, 128)], axis=1
        )
        hidden_out, back_in = gate(dot(normed, wa[...].reshape(d, 256)), dot(cot, down_main))
        rest = wr[...].reshape(d, 128)
        rest_out, rest_in = gate(dot(normed, rest), pltpu.roll(dot(cot, rest), 96, 1))
        rest_out = jnp.where(lane < 32, rest_out, 0.0)
        rest_in = jnp.where(lane < 32, rest_in, 0.0)
        at_m = slice(128 * m, 128 * (m + 1))
        bm[at_m, :] = back_in.astype(BF16)
        br[at_m, :] = rest_in.astype(BF16)
        hm[at_m, :] = hidden_out.astype(BF16)
        hr[at_m, :] = pltpu.roll(rest_out, 32, 1).astype(BF16)

    def back_side(m):
        normed = acts[2 * m].reshape(128, d)
        at_m = slice(128 * m, 128 * (m + 1))
        back_in, rest_in = bm[at_m, :], br[at_m, :]
        wide, rest = wa[...].reshape(d, 256), wr[...].reshape(d, 128)
        term = []
        step = 896
        for k in range(0, d, step):
            partial = dot_t(back_in, wide[k : k + step]) + dot_t(rest_in, rest[k : k + step])
            pb[m, :, :, :, k : k + step] = partial.astype(BF16).reshape(8, 2, 8, step)
            term.append(
                jnp.sum(partial * normed[:, k : k + step].astype(F32), axis=0, keepdims=True)
            )
        return jnp.concatenate(term, axis=1), Copy(pb.at[m, :, 1 - c], rc.at[m], rc.at[m], pair_c)

    FARTHEST_FIRST = (4, 3, 5, 2, 6, 1, 7)

    def sum_out(m, first):
        first.arrived()
        qb[m] = (pb[m, :, c].astype(F32) + rc[m].astype(F32)).astype(BF16)
        return [
            Copy(qb.at[m, mod(z + k, 8)], rz.at[m, k], rz.at[m, k], at_z(k)) for k in FARTHEST_FIRST
        ]

    def sum_in(m, parts):
        total = qb[m, z].astype(F32)
        for k, copy in zip(FARTHEST_FIRST, parts):
            copy.arrived()
            total = total + rz[m, k].astype(F32)
        st[m] = total.astype(BF16)

    def norm_side(back_normed, scaled, reciprocal, cot):
        gained = back_normed * gain_wide
        back_state = reciprocal * (
            gained - scaled * jnp.mean(gained * scaled, axis=-1, keepdims=True)
        )
        return (cot.astype(F32) + back_state).astype(BF16)

    hidden_side(0, acts[1].reshape(128, d))
    gain_term, first = back_side(0)
    parts = sum_out(0, first)
    scaled, reciprocal = scaled_of(n_s[0], n_s[1])
    sum_in(0, parts)
    hands = [
        Copy(st.at[0], nb.at[l], nb.at[l], before),
        Copy(st.at[0], nb.at[l], nb.at[1 - l], before_l),
    ]
    for copy in hands:
        copy.arrived()
    cots[z, c] = norm_side(nb[0].astype(F32) + nb[1].astype(F32), scaled, reciprocal, n_c[...])

    def cots_to_core(row):
        return Copy(cots.at[row, c], cots.at[row, c], cots.at[row, 1 - c], pair_c)

    spread = [
        Copy(cots.at[z, c], cots.at[z, c], cots.at[mod(z - k, 8), c], at_z(k)) for k in FARTHEST_FIRST
    ]
    across = [cots_to_core(z)]
    for k, copy in zip(FARTHEST_FIRST, spread):
        copy.arrived()
        across.append(cots_to_core(mod(z - k, 8)))
    for copy in across:
        copy.arrived()

    hidden_side(1, cots[...].reshape(128, d))
    ga_copies, gx_copies, gb_copies = {}, {}, {}

    def ga_step(i):
        for n, way in enumerate(DIRS):
            sub, far = GA_ITEMS[way][i]
            value = dot(xn[mod(y + way * far, 8) * 2 + (g if sub else h)], bm[...]) * scale
            if (way, sub, far + 1) in ga_copies:
                k = GA_ITEMS[way].index((sub, far + 1))
                ga_copies[way, sub, far + 1].arrived()
                value = value + gar[n, k].astype(F32)
            gas[n, i] = value.astype(BF16)
            ga_copies[way, sub, far] = Copy(gas.at[n, i], gar.at[n, i], gar.at[n, i], at_y(way))

    def ga_end(sub):
        value = dot(xn[y * 2 + (g if sub else h)], bm[...]) * scale
        for n, way in enumerate(DIRS):
            ga_copies[way, sub, 1].arrived()
            value = value + gar[n, GA_ITEMS[way].index((sub, 1))].astype(F32)
        return value

    def b_terms(far, at_h):
        k = mod(y + far, 8) * 2 + at_h
        left_n, left_c = xn[k], xc[k]
        main = dot(left_c, hm[...]) * scale
        rest = (dot(left_n, br[...]) + dot(left_c, hr[...])) * scale
        return [jnp.concatenate([main[:, 0:128], folded(rest)], axis=0), main[:, 128:256]]

    def gx_step(far):
        k = far + 3
        for j, value in enumerate(b_terms(far, g)):
            gx[j][k] = value.astype(BF16)
            gx_copies[far, j] = Copy(gx[j].at[k], hx[j].at[k], hx[j].at[k], pair_h)

    def b_pair(far):
        value = b_terms(far, h)
        for j in (0, 1):
            gx_copies[far, j].arrived()
            value[j] = value[j] + hx[j][far + 3].astype(F32)
        return value

    def gb_step(far):
        if far == 4:
            pair = b_pair(4)
        for n, way in enumerate(DIRS):
            if far < 4:
                pair = b_pair(way * far)
            for j in b_pieces(way, far, 4):
                value = pair[j]
                if (way, j, far + 1) in gb_copies:
                    gb_copies[way, j, far + 1].arrived()
                    value = value + gr[j][n, far + 1].astype(F32)
                gs[j][n, far] = value.astype(BF16)
                gb_copies[way, j, far] = Copy(
                    gs[j].at[n, far], gr[j].at[n, far], gr[j].at[n, far], at_y(way)
                )

    ga_step(0)
    ga_step(1)
    xc[:, :, 128:256] = turned(cots[...].reshape(128, d))
    for far in (4, 3, -3, 2, -2):
        gx_step(far)
    ga_step(2)
    term, first = back_side(1)
    ga[0] = (gain_term + term) * scale / gain_wide
    gain_c = Copy(ga.at[0], ga.at[1], ga.at[1], pair_c)
    for far in (1, -1, 0):
        gx_step(far)
    ga_step(3)
    gain_c.arrived()
    gz[z] = ga[0] + ga[1]
    gain_z = [Copy(gz.at[z], gz.at[z], gz.at[mod(z - k, 8)], at_z(k)) for k in FARTHEST_FIRST]
    parts = sum_out(1, first)
    gb_step(4)
    ga_step(4)
    gb_step(3)
    for copy in gain_z:
        copy.arrived()
    gy[y] = jnp.sum(gz[...], axis=0)
    gain_y = [Copy(gy.at[y], gy.at[y], gy.at[mod(y - k, 8)], at_y(k)) for k in FARTHEST_FIRST]
    ga_step(5)
    ga_step(6)
    gb_step(2)
    sum_in(1, parts)
    last = Copy(st.at[1], sr, sr, pair_l)
    fs[...] = ga_end(1).astype(BF16)
    final = Copy(fs, fr, fr, pair_h)
    for copy in gain_y:
        copy.arrived()
    mine = ga.at[2 + 2 * h + l]
    mine[...] = jnp.sum(gy[...], axis=0)
    gain_x = [
        Copy(mine, mine, ga.at[2 + 2 * h + 1 - l], pair_l),
        Copy(mine, mine, ga.at[2 + 2 * g + l], pair_h),
        Copy(mine, mine, ga.at[2 + 2 * g + 1 - l], pair_hl),
    ]
    gb_step(1)
    scaled, reciprocal = scaled_of(e_s[0, 1], e_s[1, 1])
    last.arrived()
    result = norm_side(st[1].astype(F32) + sr[...].astype(F32), scaled, reciprocal, cots[z, c])
    cot_out[0] = jnp.where(l == 0, result[0:4].astype(F32), result[4:8].astype(F32)).astype(BF16)
    for copy in gain_x:
        copy.arrived()
    gain_out[...] = ((ga[2] + ga[3]) + (ga[4] + ga[5])).reshape(d)

    up_main = ga_end(0)
    pair = b_pair(0)
    for j in (0, 1):
        for n, way in enumerate(DIRS):
            gb_copies[way, j, 1].arrived()
            pair[j] = pair[j] + gr[j][n, 1].astype(F32)
    down_out[:, 0:128] = pair[0][0:rows].astype(BF16)
    down_out[:, 128:256] = pair[1].astype(BF16)
    fold = pair[0][rows : rows + 88]
    rest = jnp.concatenate([fold, pltpu.roll(fold[0:80], 64, 1)], axis=0)
    up_out[:, 256:288] = rest[:, 0:32].astype(BF16)
    down_out[:, 256:288] = rest[:, 32:64].astype(BF16)
    final.arrived()
    up_out[:, 0:256] = (up_main + fr[...].astype(F32)).astype(BF16)

    assert len(pending) == N_COPIES, len(pending)
    for copy in pending:
        copy.out.wait_send()


def on_device(scale, saved_states, cotangent_in, lengths, gain, up_weight, down_weight):
    d = gain.shape[0]
    rows, cols = up_weight.shape
    vmem = pl.BlockSpec(memory_space=pltpu.VMEM)
    scratch = dict(
        wa=(8, 2, rows, 256), wb0=(8, 2, rows + 88, 128), wb1=(8, 2, rows, 128), wr=(8, 2, rows, 128),
        e_s=(2, 2, 4, d), e_c=(2, 4, d), n_s=(2, 4, d), n_c=(8, d), nb=(2, 8, d),
        acts=(3, 8, 2, 8, d), cots=(8, 2, 8, d), xn=(16, rows, 256), xc=(16, rows, 256),
        bm=(256, 256), hm=(256, 256), br=(256, 128), hr=(256, 128),
        pb=(2, 8, 2, 8, d), rc=(2, 8, 8, d), qb=(2, 8, 8, d), rz=(2, 8, 8, d),
        st=(2, 8, d), sr=(8, d),
        gas=(2, 7, rows, 256), gar=(2, 7, rows, 256),
        gx0=(8, rows + 88, 128), gx1=(8, rows, 128), hx0=(8, rows + 88, 128), hx1=(8, rows, 128),
        gs0=(2, 5, rows + 88, 128), gs1=(2, 5, rows, 128),
        gr0=(2, 5, rows + 88, 128), gr1=(2, 5, rows, 128),
        fs=(rows, 256), fr=(rows, 256),
    )
    outs = pl.pallas_call(
        functools.partial(kernel, scale),
        out_shape=(
            jax.ShapeDtypeStruct((1, 4, d), BF16),
            jax.ShapeDtypeStruct((rows, cols), BF16),
            jax.ShapeDtypeStruct((rows, cols), BF16),
            jax.ShapeDtypeStruct((d,), F32),
        ),
        in_specs=[vmem, vmem, pl.BlockSpec(memory_space=pltpu.SMEM), vmem, vmem, vmem],
        out_specs=(vmem,) * 4,
        scratch_shapes=[pltpu.VMEM(shape, BF16) for shape in scratch.values()]
        + [pltpu.VMEM((n, 1, d), F32) for n in (6, 8, 8)]
        + [pltpu.SemaphoreType.DMA((N_COPIES,))] * 2,
        compiler_params=pltpu.CompilerParams(
            collective_id=0, has_side_effects=True, vmem_limit_bytes=56 * 2**20
        ),
    )(saved_states, cotangent_in, lengths, gain, up_weight, down_weight.T)
    return outs[0], outs[1], outs[2].T, outs[3]


def solution(mesh):
    placed = (
        P("section", None, "dp", None),
        P("section", "dp", None),
        P("section"),
        P(),
        P("section", "dp"),
        P("dp", "section"),
    )
    scale = 1.0 / math.sqrt(2 * 128 * mesh.shape["section"])
    return jax.shard_map(
        functools.partial(on_device, scale),
        mesh=mesh,
        in_specs=placed,
        out_specs=(P("section", "dp", None), P("section", "dp"), P("dp", "section"), P()),
        check_vma=False,
    )
```

```python
import functools
import math

import jax
import jax.numpy as jnp
from jax import lax
from jax.experimental import pallas as pl
from jax.experimental.pallas import tpu as pltpu
from jax.sharding import PartitionSpec as P

MESH = pl.DeviceIdType.MESH
F32, BF16 = jnp.float32, jnp.bfloat16
epsilon = 1e-06

A_ITEMS = {
    1: ((0, 0), (1, 0), (0, 1), (1, 1), (0, 2), (1, 2), (0, 3)),
    -1: ((0, 0), (1, 0), (0, 1), (1, 1), (0, 2), (1, 2), (1, 3)),
}
GA_ITEMS = {
    1: ((0, 4), (1, 3), (0, 3), (1, 2), (0, 2), (1, 1), (0, 1)),
    -1: ((1, 4), (0, 3), (1, 3), (0, 2), (1, 2), (0, 1), (1, 1)),
}
DIRS = (1, -1)
N_OUT, N_ARRIVALS = 102, 153


def mod(a, n):
    return lax.rem(a + n, n)


def dot(a, b):
    return jnp.dot(a, b, preferred_element_type=F32)


def dot_t(a, b):
    return lax.dot_general(a, b, (((1,), (1,)), ((), ())), preferred_element_type=F32)


def b_pieces(way, far, last):
    return (0, 1) if far != last else (0,) if way == 1 else (1,)


def folded(rest):
    return jnp.concatenate([rest[0:80] + pltpu.roll(rest[88:168], 64, 1), rest[80:88]], axis=0)


def kernel(
    scale, states_in, cot_in, lengths, gain_in, up_in, down_in,
    cot_out, up_out, down_out, gain_out,
    wa, wb0, wb1, wr, e_s, e_c, n_s, n_c, nb, acts, cots, xn, xc, bm, hm, br, hr,
    pb, rc, qb, rz, st, sr,
    gas, gar, gx0, gx1, hx0, hx1, gs0, gs1, gr0, gr1, fs, fr,
    gain, up, down, slope, ga, gz, gy, send, recv, local,
):
    s, p = lax.axis_index("section"), lax.axis_index("dp")
    y, h = lax.div(s, 2), lax.rem(s, 2)
    z, l, c = lax.div(p, 4), lax.rem(lax.div(p, 2), 2), lax.rem(p, 2)
    g = 1 - h
    wb, gx, hx, gs, gr = (wb0, wb1), (gx0, gx1), (hx0, hx1), (gs0, gs1), (gr0, gr1)

    def at(section=None, dp=None):
        return {"section": s if section is None else section, "dp": p if dp is None else dp}

    def at_y(k):
        return at(section=mod(y + k, 8) * 2 + h)

    def at_z(k):
        return at(dp=mod(z + k, 8) * 4 + l * 2 + c)

    other_l = p + 2 - 4 * l
    pair_h = at(section=s + 1 - 2 * h)
    pair_l = at(dp=other_l)
    pair_c = at(dp=p + 1 - 2 * c)
    pair_hl = at(section=s + 1 - 2 * h, dp=other_l)
    before = at(section=mod(s - 1, 16))
    before_l = at(section=mod(s - 1, 16), dp=other_l)
    cross = mod(s - 1 + 2 * h, 16)

    pending = []

    arrivals, flushed, most = [0], [0], [0]

    def flush():
        for copy in pending[flushed[0] :]:
            copy.out.wait_send()
        most[0] = max(most[0], len(pending) - flushed[0])
        flushed[0] = len(pending)

    def new_arrival():
        arrivals[0] += 1
        return arrivals[0] - 1

    class Copy:
        def __init__(self, src, dst, landing, device, group=None):
            n = len(pending) - flushed[0]
            k = new_arrival() if group is None else group
            self.out = pltpu.make_async_remote_copy(
                src_ref=src, dst_ref=dst, send_sem=send.at[n], recv_sem=recv.at[k],
                device_id=device, device_id_type=MESH,
            )
            self.landing, self.k = landing, k
            pending.append(self)
            self.out.start()

        def arrived(self):
            all_arrived(self.k, self.landing)

    def all_arrived(group, landing):
        pltpu.make_async_remote_copy(
            src_ref=landing, dst_ref=landing, send_sem=send.at[0], recv_sem=recv.at[group],
            device_id=pair_c, device_id_type=MESH,
        ).wait_recv()

    barrier = pltpu.get_barrier_semaphore()
    partners = [at_y(k) for k in range(1, 8)] + [at_z(k) for k in range(1, 8)]
    partners += [pair_h, pair_l, pair_c, at(section=cross)]
    partners += [pair_hl, at(section=cross, dp=other_l)]
    for device in partners:
        pl.semaphore_signal(barrier, inc=1, device_id=device, device_id_type=MESH)

    own = [
        pltpu.make_async_copy(source, target, local.at[k])
        for k, (source, target) in enumerate(
            (
                (up_in, up), (down_in, down), (states_in.at[0], e_s.at[l]),
                (cot_in.at[0], e_c.at[l]), (gain_in, gain),
            )
        )
    ]
    for copy in own:
        copy.start()
    for copy in own:
        copy.wait()

    rows = up.shape[0]
    for j in (0, 1):
        wa[j, y, h] = up[:, 128 * j : 128 * (j + 1)]
    wb0[y, h, 0:rows, :] = down[:, 0:128]
    wb1[y, h] = down[:, 128:256]
    wb0[y, h, rows : rows + 88, :] = folded(
        jnp.concatenate(
            [up[:, 256:288].astype(F32), down[:, 256:288].astype(F32), jnp.zeros((rows, 64), F32)],
            axis=1,
        )
    ).astype(BF16)

    pl.semaphore_wait(barrier, len(partners))

    swap_s = Copy(e_s.at[l], e_s.at[l], e_s.at[1 - l], pair_l)
    swap_c = Copy(e_c.at[l], e_c.at[l], e_c.at[1 - l], pair_l)
    swap_w = [Copy(wa.at[j, y, h], wa.at[j, y, h], wa.at[j, y, g], pair_h) for j in (0, 1)]
    a_copies, b_copies = {}, {}
    x_group = [new_arrival(), new_arrival()]

    def a_step(i):
        for j in (0, 1):
            for way in DIRS:
                sub, far = A_ITEMS[way][i]
                if far > 0:
                    a_copies[way, sub, far - 1, j].arrived()
                elif sub == 1 and way == 1:
                    swap_w[j].arrived()
                row = mod(y - way * far, 8)
                land = mod(y - way * (far + 1), 8)
                at_h = g if sub else h
                block = wa.at[j, row, at_h]
                a_copies[way, sub, far, j] = Copy(block, block, wa.at[j, land, at_h], at_y(way))

    def b_across(row, j):
        Copy(wb[j].at[row, h], wb[j].at[row, h], None, pair_h, x_group[j])

    def b_step(far):
        for way in DIRS:
            row = mod(y - way * far, 8)
            land = mod(y - way * (far + 1), 8)
            for j in (0, 1):
                came = far > 0 and j in b_pieces(way, far - 1, 3)
                if came:
                    b_copies[way, j, far - 1].arrived()
                if far < 4 and j in b_pieces(way, far, 3):
                    b_copies[way, j, far] = Copy(
                        wb[j].at[row, h], wb[j].at[row, h], wb[j].at[land, h], at_y(way)
                    )
                if came:
                    b_across(row, j)

    b_step(0)
    a_step(0)
    b_across(y, 0)
    b_across(y, 1)
    b_step(1)

    d = gain.shape[0]
    gain_wide = gain[...].astype(F32).reshape(1, d)
    swap_s.arrived()
    swap_c.arrived()
    in_chunk = lax.broadcasted_iota(jnp.int32, (8, 1), 0)
    position = z * 16 + c * 4 + jnp.where(in_chunk >= 4, in_chunk + 4, in_chunk)

    def scaled_of(first, second):
        values = jnp.concatenate([first.astype(F32), second.astype(F32)], axis=0)
        reciprocal = lax.rsqrt(jnp.mean(values * values, axis=-1, keepdims=True) + epsilon)
        return values * reciprocal, reciprocal

    for m in range(2):
        acts[2 * m, z, c] = (scaled_of(e_s[0, m], e_s[1, m])[0] * gain_wide).astype(BF16)
    raw = jnp.concatenate([e_c[0].astype(F32), e_c[1].astype(F32)], axis=0)
    acts[1, z, c] = jnp.where(position < lengths[0], raw, 0.0).astype(BF16)

    FIRST, SECOND = slice(0, 2), slice(2, 3)
    z_copies, c_group = {}, new_arrival()

    def act(part, row, core):
        return acts.at[part, row, core]

    def z_send(part, k, row, far):
        row, land = mod(row, 8), mod(z - far, 8)
        z_copies[part.start, far] = Copy(act(part, row, c), act(part, row, c), act(part, land, c), at_z(k))

    def z_core(part, row):
        row = mod(row, 8)
        Copy(act(part, row, c), act(part, row, c), None, pair_c, c_group)

    def z_near(part):
        for k in (2, -2, 1, -1):
            z_send(part, k, z, k)
        z_core(part, z)

    def z_far(part):
        z_copies[part.start, 2].arrived()
        z_send(part, 2, z - 2, 4)
        z_send(part, 1, z - 2, 3)
        z_copies[part.start, -2].arrived()
        z_send(part, -1, z + 2, -3)
        for k in (2, -2, 1, -1):
            if k in (1, -1):
                z_copies[part.start, k].arrived()
            z_core(part, z - k)

    def z_last(part):
        for k in (3, -3, 4):
            z_copies[part.start, k].arrived()
            z_core(part, z - k)

    def turned(value):
        return value.astype(F32).T.astype(BF16).reshape(16, rows, 128)

    z_near(FIRST)
    a_step(1)
    z_near(SECOND)
    b_step(2)
    a_step(2)
    a_step(3)
    b_step(3)
    z_far(FIRST)
    a_step(4)
    b_step(4)
    a_step(5)
    z_far(SECOND)
    next_s = Copy(e_s.at[:, 0], n_s, n_s, before)
    next_c = Copy(acts.at[1, z, c], n_c, n_c, before)
    a_step(6)
    z_last(FIRST)
    z_last(SECOND)
    all_arrived(c_group, acts.at[:, pl.ds(0, 4)])
    xn[:, :, 0:128] = turned(acts[0].reshape(128, d))
    xn[:, :, 128:256] = turned(acts[2].reshape(128, d))
    xc[:, :, 0:128] = turned(acts[1].reshape(128, d))
    next_s.arrived()
    next_c.arrived()
    for way in DIRS:
        for sub in (0, 1):
            last = max(f for q, f in A_ITEMS[way] if q == sub)
            for j in (0, 1):
                a_copies[way, sub, last, j].arrived()
    for j in (0, 1):
        all_arrived(x_group[j], wb[j].at[pl.ds(0, 4)])
    for row in range(8):
        for k in range(2):
            fold = wb0[row, k, rows : rows + 88, :].astype(F32)
            wr[row, k] = jnp.concatenate([fold, pltpu.roll(fold[0:80], 64, 1)], axis=0).astype(BF16)

    flush()
    lane = lax.broadcasted_iota(jnp.int32, (128, 128), 1)

    def up_main():
        return jnp.concatenate([wa[0].reshape(d, 128), wa[1].reshape(d, 128)], axis=1)

    def forward_side(m):
        normed = acts[2 * m].reshape(128, d)
        hidden, hidden_rest = dot(normed, up_main()), dot(normed, wr[...].reshape(d, 128))
        sigma, sigma_rest = jax.nn.sigmoid(hidden), jax.nn.sigmoid(hidden_rest)
        at_m = slice(128 * m, 128 * (m + 1))
        hm[at_m, :] = (hidden * sigma).astype(BF16)
        rest_out = jnp.where(lane < 32, hidden_rest * sigma_rest, 0.0)
        hr[at_m, :] = pltpu.roll(rest_out, 32, 1).astype(BF16)
        slope[m, :, 0:256] = sigma * (1.0 + hidden * (1.0 - sigma))
        slope[m, :, 256:384] = sigma_rest * (1.0 + hidden_rest * (1.0 - sigma_rest))

    def hidden_side(m, cot):
        down_main = jnp.concatenate(
            [wb0[:, :, 0:rows, :].reshape(d, 128), wb1[...].reshape(d, 128)], axis=1
        )
        at_m = slice(128 * m, 128 * (m + 1))
        bm[at_m, :] = (dot(cot, down_main) * slope[m, :, 0:256]).astype(BF16)
        rest_in = pltpu.roll(dot(cot, wr[...].reshape(d, 128)), 96, 1) * slope[m, :, 256:384]
        br[at_m, :] = jnp.where(lane < 32, rest_in, 0.0).astype(BF16)

    PIECES = [(k, 896) for k in range(0, d, 896)]
    FARTHEST_FIRST = (4, 3, 5, 2, 6, 1, 7)

    def back_side(m):
        at_m = slice(128 * m, 128 * (m + 1))
        back_in, rest_in = bm[at_m, :], br[at_m, :]
        wide, rest = up_main(), wr[...].reshape(d, 128)
        normed = acts[2 * m].reshape(128, d)
        term, first = [], []
        for k, n in PIECES:
            partial = dot_t(back_in, wide[k : k + n]) + dot_t(rest_in, rest[k : k + n])
            pb[m, :, :, :, k : k + n] = partial.astype(BF16).reshape(8, 2, 8, n)
            cut = (m, slice(None), slice(None), pl.ds(k, n))
            first.append(
                Copy(pb.at[m, :, 1 - c, :, pl.ds(k, n)], rc.at[cut], rc.at[cut], pair_c)
            )
            term.append(
                jnp.sum(partial * normed[:, k : k + n].astype(F32), axis=0, keepdims=True)
            )
        return jnp.concatenate(term, axis=1), first

    def sum_out(m, first):
        groups = []
        for (k, n), copy in zip(PIECES, first):
            copy.arrived()
            qb[m, :, :, k : k + n] = (
                pb[m, :, c, :, k : k + n].astype(F32) + rc[m, :, :, k : k + n].astype(F32)
            ).astype(BF16)
            groups.append(new_arrival())
            for far in FARTHEST_FIRST:
                source, land = qb.at[m, mod(z + far, 8), :, pl.ds(k, n)], rz.at[m, far, :, pl.ds(k, n)]
                Copy(source, land, None, at_z(far), groups[-1])
        return groups

    def sum_in(m, groups):
        for (k, n), group in zip(PIECES, groups):
            all_arrived(group, rz.at[m, pl.ds(1, 7), :, pl.ds(k, n)])
            total = qb[m, z, :, k : k + n].astype(F32)
            for far in FARTHEST_FIRST:
                total = total + rz[m, far, :, k : k + n].astype(F32)
            st[m, :, k : k + n] = total.astype(BF16)

    def norm_side(back_normed, scaled, reciprocal, cot):
        gained = back_normed * gain_wide
        back_state = reciprocal * (
            gained - scaled * jnp.mean(gained * scaled, axis=-1, keepdims=True)
        )
        return (cot.astype(F32) + back_state).astype(BF16)

    forward_side(0)
    hidden_side(0, acts[1].reshape(128, d))
    gain_term, first = back_side(0)
    parts = sum_out(0, first)
    forward_side(1)
    scaled, reciprocal = scaled_of(n_s[0], n_s[1])
    sum_in(0, parts)
    hands = [
        Copy(st.at[0], nb.at[l], nb.at[l], before),
        Copy(st.at[0], nb.at[l], nb.at[1 - l], before_l),
    ]
    for copy in hands:
        copy.arrived()
    cots[z, c] = norm_side(nb[0].astype(F32) + nb[1].astype(F32), scaled, reciprocal, n_c[...])

    across = new_arrival()

    def cots_to_core(row):
        Copy(cots.at[row, c], cots.at[row, c], None, pair_c, across)

    spread = [
        Copy(cots.at[z, c], cots.at[z, c], cots.at[mod(z - k, 8), c], at_z(k)) for k in FARTHEST_FIRST
    ]
    cots_to_core(z)
    for k, copy in zip(FARTHEST_FIRST, spread):
        copy.arrived()
        cots_to_core(mod(z - k, 8))
    all_arrived(across, cots.at[pl.ds(0, 4)])

    flush()

    hidden_side(1, cots[...].reshape(128, d))
    ga_copies, gx_copies, gb_copies = {}, {}, {}

    def ga_step(i):
        values = []
        for way in DIRS:
            sub, far = GA_ITEMS[way][i]
            values.append(dot(xn[mod(y + way * far, 8) * 2 + (g if sub else h)], bm[...]) * scale)
        for j in (0, 1):
            for n, way in enumerate(DIRS):
                sub, far = GA_ITEMS[way][i]
                value = values[n][:, 128 * j : 128 * (j + 1)]
                if (way, sub, far + 1, j) in ga_copies:
                    k = GA_ITEMS[way].index((sub, far + 1))
                    ga_copies[way, sub, far + 1, j].arrived()
                    value = value + gar[n, k, j].astype(F32)
                gas[n, i, j] = value.astype(BF16)
                land = gar.at[n, i, j]
                ga_copies[way, sub, far, j] = Copy(gas.at[n, i, j], land, land, at_y(way))

    def ga_end(sub):
        value = dot(xn[y * 2 + (g if sub else h)], bm[...]) * scale
        pieces = []
        for j in (0, 1):
            piece = value[:, 128 * j : 128 * (j + 1)]
            for n, way in enumerate(DIRS):
                ga_copies[way, sub, 1, j].arrived()
                piece = piece + gar[n, GA_ITEMS[way].index((sub, 1)), j].astype(F32)
            pieces.append(piece)
        return jnp.concatenate(pieces, axis=1)

    def b_terms(far, at_h):
        k = mod(y + far, 8) * 2 + at_h
        left_n, left_c = xn[k], xc[k]
        main = dot(left_c, hm[...]) * scale
        rest = (dot(left_n, br[...]) + dot(left_c, hr[...])) * scale
        return [jnp.concatenate([main[:, 0:128], folded(rest)], axis=0), main[:, 128:256]]

    def gx_step(far):
        k = far + 3
        for j, value in enumerate(b_terms(far, g)):
            gx[j][k] = value.astype(BF16)
            gx_copies[far, j] = Copy(gx[j].at[k], hx[j].at[k], hx[j].at[k], pair_h)

    def b_pair(far):
        value = b_terms(far, h)
        for j in (0, 1):
            gx_copies[far, j].arrived()
            value[j] = value[j] + hx[j][far + 3].astype(F32)
        return value

    def gb_step(far):
        if far == 4:
            pair = b_pair(4)
        for n, way in enumerate(DIRS):
            if far < 4:
                pair = b_pair(way * far)
            for j in b_pieces(way, far, 4):
                value = pair[j]
                if (way, j, far + 1) in gb_copies:
                    gb_copies[way, j, far + 1].arrived()
                    value = value + gr[j][n, far + 1].astype(F32)
                gs[j][n, far] = value.astype(BF16)
                gb_copies[way, j, far] = Copy(
                    gs[j].at[n, far], gr[j].at[n, far], gr[j].at[n, far], at_y(way)
                )

    ga_step(0)
    xc[:, :, 128:256] = turned(cots[...].reshape(128, d))
    gx_step(4)
    ga_step(1)
    for far in (3, -3, 2, -2):
        gx_step(far)
    ga_step(2)
    term, first = back_side(1)
    ga[0] = (gain_term + term) * scale / gain_wide
    gain_c = Copy(ga.at[0], ga.at[1], ga.at[1], pair_c)
    for far in (1, -1, 0):
        gx_step(far)
    ga_step(3)
    gain_c.arrived()
    gz[z] = ga[0] + ga[1]
    gain_z = new_arrival()
    for k in FARTHEST_FIRST:
        Copy(gz.at[z], gz.at[z], None, at_z(k), gain_z)
    parts = sum_out(1, first)
    gb_step(4)
    ga_step(4)
    gb_step(3)
    all_arrived(gain_z, gz.at[pl.ds(0, 7)])
    gy[y] = jnp.sum(gz[...], axis=0)
    gain_y = new_arrival()
    for k in FARTHEST_FIRST:
        Copy(gy.at[y], gy.at[y], None, at_y(k), gain_y)
    ga_step(5)
    ga_step(6)
    gb_step(2)
    sum_in(1, parts)
    last = Copy(st.at[1], sr, sr, pair_l)
    fs[...] = ga_end(1).astype(BF16)
    final = Copy(fs, fr, fr, pair_h)
    all_arrived(gain_y, gy.at[pl.ds(0, 7)])
    mine = ga.at[2 + 2 * h + l]
    mine[...] = jnp.sum(gy[...], axis=0)
    gain_x = [
        Copy(mine, mine, ga.at[2 + 2 * h + 1 - l], pair_l),
        Copy(mine, mine, ga.at[2 + 2 * g + l], pair_h),
        Copy(mine, mine, ga.at[2 + 2 * g + 1 - l], pair_hl),
    ]
    gb_step(1)
    scaled, reciprocal = scaled_of(e_s[0, 1], e_s[1, 1])
    last.arrived()
    result = norm_side(st[1].astype(F32) + sr[...].astype(F32), scaled, reciprocal, cots[z, c])
    cot_out[0] = jnp.where(l == 0, result[0:4].astype(F32), result[4:8].astype(F32)).astype(BF16)
    for copy in gain_x:
        copy.arrived()
    gain_out[...] = ((ga[2] + ga[3]) + (ga[4] + ga[5])).reshape(d)

    up_sum = ga_end(0)
    pair = b_pair(0)
    for j in (0, 1):
        for n, way in enumerate(DIRS):
            gb_copies[way, j, 1].arrived()
            pair[j] = pair[j] + gr[j][n, 1].astype(F32)
    down_out[:, 0:128] = pair[0][0:rows].astype(BF16)
    down_out[:, 128:256] = pair[1].astype(BF16)
    fold = pair[0][rows : rows + 88]
    rest = jnp.concatenate([fold, pltpu.roll(fold[0:80], 64, 1)], axis=0)
    up_out[:, 256:288] = rest[:, 0:32].astype(BF16)
    down_out[:, 256:288] = rest[:, 32:64].astype(BF16)
    final.arrived()
    up_out[:, 0:256] = (up_sum + fr[...].astype(F32)).astype(BF16)

    flush()
    assert (most[0], arrivals[0]) == (N_OUT, N_ARRIVALS), (most, arrivals)


def on_device(scale, saved_states, cotangent_in, lengths, gain, up_weight, down_weight):
    d = gain.shape[0]
    rows, cols = up_weight.shape
    vmem = pl.BlockSpec(memory_space=pltpu.VMEM)
    there = pl.BlockSpec(memory_space=pl.ANY)
    scratch = dict(
        wa=(2, 8, 2, rows, 128), wb0=(8, 2, rows + 88, 128), wb1=(8, 2, rows, 128), wr=(8, 2, rows, 128),
        e_s=(2, 2, 4, d), e_c=(2, 4, d), n_s=(2, 4, d), n_c=(8, d), nb=(2, 8, d),
        acts=(3, 8, 2, 8, d), cots=(8, 2, 8, d), xn=(16, rows, 256), xc=(16, rows, 256),
        bm=(256, 256), hm=(256, 256), br=(256, 128), hr=(256, 128),
        pb=(2, 8, 2, 8, d), rc=(2, 8, 8, d), qb=(2, 8, 8, d), rz=(2, 8, 8, d),
        st=(2, 8, d), sr=(8, d),
        gas=(2, 7, 2, rows, 128), gar=(2, 7, 2, rows, 128),
        gx0=(8, rows + 88, 128), gx1=(8, rows, 128), hx0=(8, rows + 88, 128), hx1=(8, rows, 128),
        gs0=(2, 5, rows + 88, 128), gs1=(2, 5, rows, 128),
        gr0=(2, 5, rows + 88, 128), gr1=(2, 5, rows, 128),
        fs=(rows, 256), fr=(rows, 256),
    )
    outs = pl.pallas_call(
        functools.partial(kernel, scale),
        out_shape=(
            jax.ShapeDtypeStruct((1, 4, d), BF16),
            jax.ShapeDtypeStruct((rows, cols), BF16),
            jax.ShapeDtypeStruct((rows, cols), BF16),
            jax.ShapeDtypeStruct((d,), F32),
        ),
        in_specs=[there, there, pl.BlockSpec(memory_space=pltpu.SMEM), there, there, there],
        out_specs=(vmem,) * 4,
        scratch_shapes=[pltpu.VMEM(shape, BF16) for shape in scratch.values()]
        + [pltpu.VMEM((d,), BF16)]
        + [pltpu.VMEM((rows, cols), BF16)] * 2
        + [pltpu.VMEM((2, 128, 384), F32)]
        + [pltpu.VMEM((n, 1, d), F32) for n in (6, 8, 8)]
        + [pltpu.SemaphoreType.DMA((n,)) for n in (N_OUT, N_ARRIVALS, 5)],
        compiler_params=pltpu.CompilerParams(
            collective_id=0, has_side_effects=True, vmem_limit_bytes=56 * 2**20
        ),
    )(saved_states, cotangent_in, lengths, gain, up_weight, down_weight.T)
    return outs[0], outs[1], outs[2].T, outs[3]


def solution(mesh):
    placed = (
        P("section", None, "dp", None),
        P("section", "dp", None),
        P("section"),
        P(),
        P("section", "dp"),
        P("dp", "section"),
    )
    scale = 1.0 / math.sqrt(2 * 128 * mesh.shape["section"])
    return jax.shard_map(
        functools.partial(on_device, scale),
        mesh=mesh,
        in_specs=placed,
        out_specs=(P("section", "dp", None), P("section", "dp"), P("dp", "section"), P()),
        check_vma=False,
    )
```

```python
import functools
import math

import jax
import jax.numpy as jnp
from jax import lax
from jax.experimental import pallas as pl
from jax.experimental.pallas import tpu as pltpu
from jax.sharding import PartitionSpec as P

MESH = pl.DeviceIdType.MESH
F32, BF16 = jnp.float32, jnp.bfloat16
epsilon = 1e-06

A_ITEMS = {
    1: ((0, 0), (1, 0), (0, 1), (1, 1), (0, 2), (1, 2), (0, 3)),
    -1: ((0, 0), (1, 0), (0, 1), (1, 1), (0, 2), (1, 2), (1, 3)),
}
GA_ITEMS = {
    1: ((0, 4), (1, 3), (0, 3), (1, 2), (0, 2), (1, 1), (0, 1)),
    -1: ((1, 4), (0, 3), (1, 3), (0, 2), (1, 2), (0, 1), (1, 1)),
}
DIRS = (1, -1)
N_OUT, N_ARRIVALS = 102, 153


def mod(a, n):
    return lax.rem(a + n, n)


def dot(a, b):
    return jnp.dot(a, b, preferred_element_type=F32)


def dot_t(a, b):
    return lax.dot_general(a, b, (((1,), (1,)), ((), ())), preferred_element_type=F32)


def b_pieces(way, far, last):
    return (0, 1) if far != last else (0,) if way == 1 else (1,)


def folded(rest):
    return jnp.concatenate([rest[0:80] + pltpu.roll(rest[88:168], 64, 1), rest[80:88]], axis=0)


def kernel(
    scale, states_in, cot_in, lengths, gain_in, up_in, down_in,
    cot_out, up_out, down_out, gain_out,
    wa, wb0, wb1, wr, e_s, e_c, n_s, n_c, nb, acts, cots, xn, xc, bm, hm, br, hr,
    pb, rc, qb, rz, st, sr,
    gas, gar, gx0, gx1, hx0, hx1, gs0, gs1, gr0, gr1, fs, fr,
    gain, up, down, slope, ga, gz, gy, send, recv, local,
):
    s, p = lax.axis_index("section"), lax.axis_index("dp")
    y, h = lax.div(s, 2), lax.rem(s, 2)
    z, l, c = lax.div(p, 4), lax.rem(lax.div(p, 2), 2), lax.rem(p, 2)
    g = 1 - h
    wb, gx, hx, gs, gr = (wb0, wb1), (gx0, gx1), (hx0, hx1), (gs0, gs1), (gr0, gr1)

    def at(section=None, dp=None):
        return {"section": s if section is None else section, "dp": p if dp is None else dp}

    def at_y(k):
        return at(section=mod(y + k, 8) * 2 + h)

    def at_z(k):
        return at(dp=mod(z + k, 8) * 4 + l * 2 + c)

    other_l = p + 2 - 4 * l
    pair_h = at(section=s + 1 - 2 * h)
    pair_l = at(dp=other_l)
    pair_c = at(dp=p + 1 - 2 * c)
    pair_hl = at(section=s + 1 - 2 * h, dp=other_l)
    before = at(section=mod(s - 1, 16))
    before_l = at(section=mod(s - 1, 16), dp=other_l)
    cross = mod(s - 1 + 2 * h, 16)

    pending = []

    arrivals, flushed, most = [0], [0], [0]

    def flush():
        for copy in pending[flushed[0] :]:
            copy.out.wait_send()
        most[0] = max(most[0], len(pending) - flushed[0])
        flushed[0] = len(pending)

    def new_arrival():
        arrivals[0] += 1
        return arrivals[0] - 1

    class Copy:
        def __init__(self, src, dst, landing, device, group=None):
            n = len(pending) - flushed[0]
            k = new_arrival() if group is None else group
            self.out = pltpu.make_async_remote_copy(
                src_ref=src, dst_ref=dst, send_sem=send.at[n], recv_sem=recv.at[k],
                device_id=device, device_id_type=MESH,
            )
            self.landing, self.k = landing, k
            pending.append(self)
            self.out.start()

        def arrived(self):
            all_arrived(self.k, self.landing)

    def all_arrived(group, landing):
        pltpu.make_async_remote_copy(
            src_ref=landing, dst_ref=landing, send_sem=send.at[0], recv_sem=recv.at[group],
            device_id=pair_c, device_id_type=MESH,
        ).wait_recv()

    barrier = pltpu.get_barrier_semaphore()
    partners = [at_y(k) for k in range(1, 8)] + [at_z(k) for k in range(1, 8)]
    partners += [pair_h, pair_l, pair_c, at(section=cross)]
    partners += [pair_hl, at(section=cross, dp=other_l)]
    for device in partners:
        pl.semaphore_signal(barrier, inc=1, device_id=device, device_id_type=MESH)

    own = [
        pltpu.make_async_copy(source, target, local.at[k])
        for k, (source, target) in enumerate(
            (
                (up_in, up), (down_in, down), (states_in.at[0], e_s.at[l]),
                (cot_in.at[0], e_c.at[l]), (gain_in, gain),
            )
        )
    ]
    for copy in own:
        copy.start()
    for copy in own:
        copy.wait()

    rows = up.shape[0]
    for j in (0, 1):
        wa[j, y, h] = up[:, 128 * j : 128 * (j + 1)]
    wb0[y, h, 0:rows, :] = down[:, 0:128]
    wb1[y, h] = down[:, 128:256]
    wb0[y, h, rows : rows + 88, :] = folded(
        jnp.concatenate(
            [up[:, 256:288].astype(F32), down[:, 256:288].astype(F32), jnp.zeros((rows, 64), F32)],
            axis=1,
        )
    ).astype(BF16)

    pl.semaphore_wait(barrier, len(partners))

    swap_s = Copy(e_s.at[l], e_s.at[l], e_s.at[1 - l], pair_l)
    swap_c = Copy(e_c.at[l], e_c.at[l], e_c.at[1 - l], pair_l)
    swap_w = [Copy(wa.at[j, y, h], wa.at[j, y, h], wa.at[j, y, g], pair_h) for j in (0, 1)]
    a_copies, b_copies = {}, {}
    x_group = [new_arrival(), new_arrival()]

    def a_step(i):
        for j in (0, 1):
            for way in DIRS:
                sub, far = A_ITEMS[way][i]
                if far > 0:
                    a_copies[way, sub, far - 1, j].arrived()
                elif sub == 1 and way == 1:
                    swap_w[j].arrived()
                row = mod(y - way * far, 8)
                land = mod(y - way * (far + 1), 8)
                at_h = g if sub else h
                block = wa.at[j, row, at_h]
                a_copies[way, sub, far, j] = Copy(block, block, wa.at[j, land, at_h], at_y(way))

    def b_across(row, j):
        Copy(wb[j].at[row, h], wb[j].at[row, h], None, pair_h, x_group[j])

    def b_step(far):
        for way in DIRS:
            row = mod(y - way * far, 8)
            land = mod(y - way * (far + 1), 8)
            for j in (0, 1):
                came = far > 0 and j in b_pieces(way, far - 1, 3)
                if came:
                    b_copies[way, j, far - 1].arrived()
                if far < 4 and j in b_pieces(way, far, 3):
                    b_copies[way, j, far] = Copy(
                        wb[j].at[row, h], wb[j].at[row, h], wb[j].at[land, h], at_y(way)
                    )
                if came:
                    b_across(row, j)

    b_step(0)
    a_step(0)
    b_across(y, 0)
    b_across(y, 1)
    b_step(1)

    d = gain.shape[0]
    gain_wide = gain[...].astype(F32).reshape(1, d)
    swap_s.arrived()
    swap_c.arrived()
    in_chunk = lax.broadcasted_iota(jnp.int32, (8, 1), 0)
    position = z * 16 + c * 4 + jnp.where(in_chunk >= 4, in_chunk + 4, in_chunk)

    def scaled_of(first, second):
        values = jnp.concatenate([first.astype(F32), second.astype(F32)], axis=0)
        reciprocal = lax.rsqrt(jnp.mean(values * values, axis=-1, keepdims=True) + epsilon)
        return values * reciprocal, reciprocal

    for m in range(2):
        acts[2 * m, z, c] = (scaled_of(e_s[0, m], e_s[1, m])[0] * gain_wide).astype(BF16)
    raw = jnp.concatenate([e_c[0].astype(F32), e_c[1].astype(F32)], axis=0)
    acts[1, z, c] = jnp.where(position < lengths[0], raw, 0.0).astype(BF16)

    FIRST, SECOND = slice(0, 2), slice(2, 3)
    z_copies, c_group = {}, new_arrival()

    def act(part, row, core):
        return acts.at[part, row, core]

    def z_send(part, k, row, far):
        row, land = mod(row, 8), mod(z - far, 8)
        z_copies[part.start, far] = Copy(act(part, row, c), act(part, row, c), act(part, land, c), at_z(k))

    def z_core(part, row):
        row = mod(row, 8)
        Copy(act(part, row, c), act(part, row, c), None, pair_c, c_group)

    def z_near(part):
        for k in (2, -2, 1, -1):
            z_send(part, k, z, k)
        z_core(part, z)

    def z_far(part):
        z_copies[part.start, 2].arrived()
        z_send(part, 2, z - 2, 4)
        z_send(part, 1, z - 2, 3)
        z_copies[part.start, -2].arrived()
        z_send(part, -1, z + 2, -3)
        for k in (2, -2, 1, -1):
            if k in (1, -1):
                z_copies[part.start, k].arrived()
            z_core(part, z - k)

    def z_last(part):
        for k in (3, -3, 4):
            z_copies[part.start, k].arrived()
            z_core(part, z - k)

    def turned(value):
        return value.astype(F32).T.astype(BF16).reshape(16, rows, 128)

    z_near(FIRST)
    a_step(1)
    z_near(SECOND)
    b_step(2)
    a_step(2)
    a_step(3)
    b_step(3)
    z_far(FIRST)
    a_step(4)
    b_step(4)
    a_step(5)
    z_far(SECOND)
    next_s = Copy(e_s.at[:, 0], n_s, n_s, before)
    next_c = Copy(acts.at[1, z, c], n_c, n_c, before)
    a_step(6)
    z_last(FIRST)
    z_last(SECOND)
    all_arrived(c_group, acts.at[:, pl.ds(0, 4)])
    next_s.arrived()
    next_c.arrived()
    for way in DIRS:
        for sub in (0, 1):
            last = max(f for q, f in A_ITEMS[way] if q == sub)
            for j in (0, 1):
                a_copies[way, sub, last, j].arrived()
    for j in (0, 1):
        all_arrived(x_group[j], wb[j].at[pl.ds(0, 4)])
    for row in range(8):
        for k in range(2):
            fold = wb0[row, k, rows : rows + 88, :].astype(F32)
            wr[row, k] = jnp.concatenate([fold, pltpu.roll(fold[0:80], 64, 1)], axis=0).astype(BF16)

    flush()
    lane = lax.broadcasted_iota(jnp.int32, (128, 128), 1)

    def up_main():
        return jnp.concatenate([wa[0].reshape(d, 128), wa[1].reshape(d, 128)], axis=1)

    def forward_side(m):
        normed = acts[2 * m].reshape(128, d)
        hidden, hidden_rest = dot(normed, up_main()), dot(normed, wr[...].reshape(d, 128))
        sigma, sigma_rest = jax.nn.sigmoid(hidden), jax.nn.sigmoid(hidden_rest)
        at_m = slice(128 * m, 128 * (m + 1))
        hm[at_m, :] = (hidden * sigma).astype(BF16)
        rest_out = jnp.where(lane < 32, hidden_rest * sigma_rest, 0.0)
        hr[at_m, :] = pltpu.roll(rest_out, 32, 1).astype(BF16)
        slope[m, :, 0:256] = sigma * (1.0 + hidden * (1.0 - sigma))
        slope[m, :, 256:384] = sigma_rest * (1.0 + hidden_rest * (1.0 - sigma_rest))

    def hidden_side(m, cot):
        down_main = jnp.concatenate(
            [wb0[:, :, 0:rows, :].reshape(d, 128), wb1[...].reshape(d, 128)], axis=1
        )
        at_m = slice(128 * m, 128 * (m + 1))
        bm[at_m, :] = (dot(cot, down_main) * slope[m, :, 0:256]).astype(BF16)
        rest_in = pltpu.roll(dot(cot, wr[...].reshape(d, 128)), 96, 1) * slope[m, :, 256:384]
        br[at_m, :] = jnp.where(lane < 32, rest_in, 0.0).astype(BF16)

    PIECES = [(k, 896) for k in range(0, d, 896)]
    FARTHEST_FIRST = (4, 3, 5, 2, 6, 1, 7)

    def back_side(m):
        at_m = slice(128 * m, 128 * (m + 1))
        back_in, rest_in = bm[at_m, :], br[at_m, :]
        wide, rest = up_main(), wr[...].reshape(d, 128)
        normed = acts[2 * m].reshape(128, d)
        term, first = [], []
        for k, n in PIECES:
            partial = dot_t(back_in, wide[k : k + n]) + dot_t(rest_in, rest[k : k + n])
            pb[m, :, :, :, k : k + n] = partial.astype(BF16).reshape(8, 2, 8, n)
            cut = (m, slice(None), slice(None), pl.ds(k, n))
            first.append(
                Copy(pb.at[m, :, 1 - c, :, pl.ds(k, n)], rc.at[cut], rc.at[cut], pair_c)
            )
            term.append(
                jnp.sum(partial * normed[:, k : k + n].astype(F32), axis=0, keepdims=True)
            )
        return jnp.concatenate(term, axis=1), first

    def sum_out(m, first):
        groups = []
        for (k, n), copy in zip(PIECES, first):
            copy.arrived()
            qb[m, :, :, k : k + n] = (
                pb[m, :, c, :, k : k + n].astype(F32) + rc[m, :, :, k : k + n].astype(F32)
            ).astype(BF16)
            groups.append(new_arrival())
            for far in FARTHEST_FIRST:
                source, land = qb.at[m, mod(z + far, 8), :, pl.ds(k, n)], rz.at[m, far, :, pl.ds(k, n)]
                Copy(source, land, None, at_z(far), groups[-1])
        return groups

    def sum_in(m, groups):
        for (k, n), group in zip(PIECES, groups):
            all_arrived(group, rz.at[m, pl.ds(1, 7), :, pl.ds(k, n)])
            total = qb[m, z, :, k : k + n].astype(F32)
            for far in FARTHEST_FIRST:
                total = total + rz[m, far, :, k : k + n].astype(F32)
            st[m, :, k : k + n] = total.astype(BF16)

    def norm_side(back_normed, scaled, reciprocal, cot):
        gained = back_normed * gain_wide
        back_state = reciprocal * (
            gained - scaled * jnp.mean(gained * scaled, axis=-1, keepdims=True)
        )
        return (cot.astype(F32) + back_state).astype(BF16)

    forward_side(0)
    hidden_side(0, acts[1].reshape(128, d))
    gain_term, first = back_side(0)
    parts = sum_out(0, first)
    forward_side(1)
    xn[:, :, 0:128] = turned(acts[0].reshape(128, d))
    xn[:, :, 128:256] = turned(acts[2].reshape(128, d))
    xc[:, :, 0:128] = turned(acts[1].reshape(128, d))
    scaled, reciprocal = scaled_of(n_s[0], n_s[1])
    sum_in(0, parts)
    hands = [
        Copy(st.at[0], nb.at[l], nb.at[l], before),
        Copy(st.at[0], nb.at[l], nb.at[1 - l], before_l),
    ]
    for copy in hands:
        copy.arrived()
    cots[z, c] = norm_side(nb[0].astype(F32) + nb[1].astype(F32), scaled, reciprocal, n_c[...])

    across = new_arrival()

    def cots_to_core(row):
        Copy(cots.at[row, c], cots.at[row, c], None, pair_c, across)

    spread = [
        Copy(cots.at[z, c], cots.at[z, c], cots.at[mod(z - k, 8), c], at_z(k)) for k in FARTHEST_FIRST
    ]
    cots_to_core(z)
    for k, copy in zip(FARTHEST_FIRST, spread):
        copy.arrived()
        cots_to_core(mod(z - k, 8))
    all_arrived(across, cots.at[pl.ds(0, 4)])

    flush()

    hidden_side(1, cots[...].reshape(128, d))
    ga_copies, gx_copies, gb_copies = {}, {}, {}

    def ga_step(i):
        values = []
        for way in DIRS:
            sub, far = GA_ITEMS[way][i]
            values.append(dot(xn[mod(y + way * far, 8) * 2 + (g if sub else h)], bm[...]) * scale)
        for j in (0, 1):
            for n, way in enumerate(DIRS):
                sub, far = GA_ITEMS[way][i]
                value = values[n][:, 128 * j : 128 * (j + 1)]
                if (way, sub, far + 1, j) in ga_copies:
                    k = GA_ITEMS[way].index((sub, far + 1))
                    ga_copies[way, sub, far + 1, j].arrived()
                    value = value + gar[n, k, j].astype(F32)
                gas[n, i, j] = value.astype(BF16)
                land = gar.at[n, i, j]
                ga_copies[way, sub, far, j] = Copy(gas.at[n, i, j], land, land, at_y(way))

    def ga_end(sub):
        value = dot(xn[y * 2 + (g if sub else h)], bm[...]) * scale
        pieces = []
        for j in (0, 1):
            piece = value[:, 128 * j : 128 * (j + 1)]
            for n, way in enumerate(DIRS):
                ga_copies[way, sub, 1, j].arrived()
                piece = piece + gar[n, GA_ITEMS[way].index((sub, 1)), j].astype(F32)
            pieces.append(piece)
        return jnp.concatenate(pieces, axis=1)

    def b_terms(far, at_h):
        k = mod(y + far, 8) * 2 + at_h
        left_n, left_c = xn[k], xc[k]
        main = dot(left_c, hm[...]) * scale
        rest = (dot(left_n, br[...]) + dot(left_c, hr[...])) * scale
        return [jnp.concatenate([main[:, 0:128], folded(rest)], axis=0), main[:, 128:256]]

    def gx_step(far):
        k = far + 3
        for j, value in enumerate(b_terms(far, g)):
            gx[j][k] = value.astype(BF16)
            gx_copies[far, j] = Copy(gx[j].at[k], hx[j].at[k], hx[j].at[k], pair_h)

    def b_pair(far):
        value = b_terms(far, h)
        for j in (0, 1):
            gx_copies[far, j].arrived()
            value[j] = value[j] + hx[j][far + 3].astype(F32)
        return value

    def gb_step(far):
        if far == 4:
            pair = b_pair(4)
        for n, way in enumerate(DIRS):
            if far < 4:
                pair = b_pair(way * far)
            for j in b_pieces(way, far, 4):
                value = pair[j]
                if (way, j, far + 1) in gb_copies:
                    gb_copies[way, j, far + 1].arrived()
                    value = value + gr[j][n, far + 1].astype(F32)
                gs[j][n, far] = value.astype(BF16)
                gb_copies[way, j, far] = Copy(
                    gs[j].at[n, far], gr[j].at[n, far], gr[j].at[n, far], at_y(way)
                )

    ga_step(0)
    xc[:, :, 128:256] = turned(cots[...].reshape(128, d))
    gx_step(4)
    ga_step(1)
    for far in (3, -3, 2, -2):
        gx_step(far)
    ga_step(2)
    term, first = back_side(1)
    ga[0] = (gain_term + term) * scale / gain_wide
    gain_c = Copy(ga.at[0], ga.at[1], ga.at[1], pair_c)
    for far in (1, -1, 0):
        gx_step(far)
    ga_step(3)
    gain_c.arrived()
    gz[z] = ga[0] + ga[1]
    gain_z = new_arrival()
    for k in FARTHEST_FIRST:
        Copy(gz.at[z], gz.at[z], None, at_z(k), gain_z)
    parts = sum_out(1, first)
    gb_step(4)
    ga_step(4)
    all_arrived(gain_z, gz.at[pl.ds(0, 7)])
    gy[y] = jnp.sum(gz[...], axis=0)
    gain_y = new_arrival()
    for k in FARTHEST_FIRST:
        Copy(gy.at[y], gy.at[y], None, at_y(k), gain_y)
    gb_step(3)
    ga_step(5)
    ga_step(6)
    gb_step(2)
    sum_in(1, parts)
    last = Copy(st.at[1], sr, sr, pair_l)
    all_arrived(gain_y, gy.at[pl.ds(0, 7)])
    mine = ga.at[2 + 2 * h + l]
    mine[...] = jnp.sum(gy[...], axis=0)
    gain_x = [
        Copy(mine, mine, ga.at[2 + 2 * h + 1 - l], pair_l),
        Copy(mine, mine, ga.at[2 + 2 * g + l], pair_h),
        Copy(mine, mine, ga.at[2 + 2 * g + 1 - l], pair_hl),
    ]
    fs[...] = ga_end(1).astype(BF16)
    final = Copy(fs, fr, fr, pair_h)
    gb_step(1)
    scaled, reciprocal = scaled_of(e_s[0, 1], e_s[1, 1])
    last.arrived()
    result = norm_side(st[1].astype(F32) + sr[...].astype(F32), scaled, reciprocal, cots[z, c])
    cot_out[0] = jnp.where(l == 0, result[0:4].astype(F32), result[4:8].astype(F32)).astype(BF16)
    for copy in gain_x:
        copy.arrived()
    gain_out[...] = ((ga[2] + ga[3]) + (ga[4] + ga[5])).reshape(d)

    up_sum = ga_end(0)
    pair = b_pair(0)
    for j in (0, 1):
        for n, way in enumerate(DIRS):
            gb_copies[way, j, 1].arrived()
            pair[j] = pair[j] + gr[j][n, 1].astype(F32)
    down_out[:, 0:128] = pair[0][0:rows].astype(BF16)
    down_out[:, 128:256] = pair[1].astype(BF16)
    fold = pair[0][rows : rows + 88]
    rest = jnp.concatenate([fold, pltpu.roll(fold[0:80], 64, 1)], axis=0)
    up_out[:, 256:288] = rest[:, 0:32].astype(BF16)
    down_out[:, 256:288] = rest[:, 32:64].astype(BF16)
    final.arrived()
    up_out[:, 0:256] = (up_sum + fr[...].astype(F32)).astype(BF16)

    flush()
    assert (most[0], arrivals[0]) == (N_OUT, N_ARRIVALS), (most, arrivals)


def on_device(scale, saved_states, cotangent_in, lengths, gain, up_weight, down_weight):
    d = gain.shape[0]
    rows, cols = up_weight.shape
    vmem = pl.BlockSpec(memory_space=pltpu.VMEM)
    there = pl.BlockSpec(memory_space=pl.ANY)
    scratch = dict(
        wa=(2, 8, 2, rows, 128), wb0=(8, 2, rows + 88, 128), wb1=(8, 2, rows, 128), wr=(8, 2, rows, 128),
        e_s=(2, 2, 4, d), e_c=(2, 4, d), n_s=(2, 4, d), n_c=(8, d), nb=(2, 8, d),
        acts=(3, 8, 2, 8, d), cots=(8, 2, 8, d), xn=(16, rows, 256), xc=(16, rows, 256),
        bm=(256, 256), hm=(256, 256), br=(256, 128), hr=(256, 128),
        pb=(2, 8, 2, 8, d), rc=(2, 8, 8, d), qb=(2, 8, 8, d), rz=(2, 8, 8, d),
        st=(2, 8, d), sr=(8, d),
        gas=(2, 7, 2, rows, 128), gar=(2, 7, 2, rows, 128),
        gx0=(8, rows + 88, 128), gx1=(8, rows, 128), hx0=(8, rows + 88, 128), hx1=(8, rows, 128),
        gs0=(2, 5, rows + 88, 128), gs1=(2, 5, rows, 128),
        gr0=(2, 5, rows + 88, 128), gr1=(2, 5, rows, 128),
        fs=(rows, 256), fr=(rows, 256),
    )
    outs = pl.pallas_call(
        functools.partial(kernel, scale),
        out_shape=(
            jax.ShapeDtypeStruct((1, 4, d), BF16),
            jax.ShapeDtypeStruct((rows, cols), BF16),
            jax.ShapeDtypeStruct((rows, cols), BF16),
            jax.ShapeDtypeStruct((d,), F32),
        ),
        in_specs=[there, there, pl.BlockSpec(memory_space=pltpu.SMEM), there, there, there],
        out_specs=(vmem,) * 4,
        scratch_shapes=[pltpu.VMEM(shape, BF16) for shape in scratch.values()]
        + [pltpu.VMEM((d,), BF16)]
        + [pltpu.VMEM((rows, cols), BF16)] * 2
        + [pltpu.VMEM((2, 128, 384), F32)]
        + [pltpu.VMEM((n, 1, d), F32) for n in (6, 8, 8)]
        + [pltpu.SemaphoreType.DMA((n,)) for n in (N_OUT, N_ARRIVALS, 5)],
        compiler_params=pltpu.CompilerParams(
            collective_id=0, has_side_effects=True, vmem_limit_bytes=56 * 2**20
        ),
    )(saved_states, cotangent_in, lengths, gain, up_weight, down_weight.T)
    return outs[0], outs[1], outs[2].T, outs[3]


def solution(mesh):
    placed = (
        P("section", None, "dp", None),
        P("section", "dp", None),
        P("section"),
        P(),
        P("section", "dp"),
        P("dp", "section"),
    )
    scale = 1.0 / math.sqrt(2 * 128 * mesh.shape["section"])
    return jax.shard_map(
        functools.partial(on_device, scale),
        mesh=mesh,
        in_specs=placed,
        out_specs=(P("section", "dp", None), P("section", "dp"), P("dp", "section"), P()),
        check_vma=False,
    )
```
